256 devices in a mesh: grp: 16 (over y, x), seq: 16 (over z, core).
Axes of the slice: x: 4, y: 4, z: 8, core: 2. Of those that a mesh axis runs over, the one named last changes fastest.
Arguments:
- inputs: bfloat16 [65536, 2560], P(('grp', 'seq')), may hold values from -0.03125 to 0.03125
- out_grad: bfloat16 [65536, 2560], P(('grp', 'seq')), may hold values from -6 to 6
- input_map: bfloat16 [65536, 128], P(('grp', 'seq')), may hold values from -0.09375 to 0.09375
- output_map: bfloat16 [65536, 128], P(('grp', 'seq')), may hold values from -0.09375 to 0.09375
- log_decay: float32 [40, 65536], P(None, ('grp', 'seq')), may hold values from -1 to 0, as said below
Outputs:
- grad_inputs: bfloat16 [65536, 2560], P(('grp', 'seq'))
- grad_input_map: bfloat16 [65536, 128], P(('grp', 'seq'))
- grad_output_map: bfloat16 [65536, 128], P(('grp', 'seq'))
- grad_decay: float32 [40, 65536], P(None, ('grp', 'seq'))
The draws below stay inside these ranges and needn't reach their ends.
Inputs may be any that keep to these rules, and one draw needn't show every extreme that they name: log_decay is negative everywhere.
All inputs are finite; a program needn't handle non-finite values.
Results may differ from the reference program's by a relative error of at most 0.0081.
Values sent between devices are 32-bit elements; how exact they have to be, the bound alone decides.
A program may use at most 192 MiB of HBM per device.

```python
import math
import jax
import jax.numpy as jnp
from jax import lax

HEADS = 40
HEADDIM = 64
STATE = 128
STRETCH = 256
TOKENS = 65536


def draw_log_decay(key, part):
    keys = jax.random.split(jax.random.fold_in(key, 11), 6)
    fast_share = 0.5
    picked = jax.random.uniform(keys[0], (HEADS, 1), jnp.float32) < fast_share
    fast_rate = jnp.minimum(jnp.exp(jax.random.uniform(keys[1], (HEADS, 1), jnp.float32, math.log(5.0), math.log(8.0))) / STRETCH, 0.15)
    slow_rate = jnp.exp(jax.random.uniform(keys[2], (HEADS, 1), jnp.float32, math.log(0.05), math.log(0.5))) * 2.3 / TOKENS
    baseline_decay_rate = jnp.where(picked, fast_rate, slow_rate)
    coarse_estimate = jnp.exp(jax.random.uniform(keys[3], (HEADS, TOKENS), jnp.float32, -math.log(2.0), math.log(2.0)))
    marked_positions = jax.random.randint(keys[4], (HEADS, 3), 0, TOKENS)
    position_slots = jnp.arange(TOKENS, dtype=jnp.int32)
    sudden_jump = jnp.any(position_slots[None, None, :] == marked_positions[:, :, None], axis=1)
    layer_depth_count = jax.random.uniform(keys[5], (HEADS, TOKENS), jnp.float32, 0.22, 0.69)
    return -(baseline_decay_rate * coarse_estimate) - jnp.where(sudden_jump, layer_depth_count, 0.0)


def levels(rng, extent, cuts, low, high):
    gain = 1.0
    for axis_at, shards_of in cuts:
        heights = jax.random.uniform(jax.random.fold_in(jax.random.fold_in(rng, 6), axis_at), (shards_of,), jnp.float32, low / len(cuts), high / len(cuts))
        gain = gain * jnp.repeat(jnp.exp(heights), extent[axis_at] // shards_of).reshape((-1,) + (1,) * (len(extent) - 1 - axis_at))
    return gain


def bell_draw(own_key, shape, width, reach, shards=(), kind=jnp.bfloat16):
    array = jax.random.normal(own_key, shape, jnp.float32) * width
    if len(shards) > 0:
        array = levels(own_key, shape, shards, -0.22, 0.18) * array
    return jnp.clip(array, min=-reach, max=reach).astype(kind)


def setup_inputs(seed: int = 0) -> dict:
    streams_of = jax.random.split(jax.random.key(seed), 6)
    return {
        "inputs": bell_draw(streams_of[0], (TOKENS, HEADS * HEADDIM), (TOKENS * HEADS * HEADDIM // (32 * STATE)) ** -0.5, 0.03125, ((0, 256),)),
        "out_grad": bell_draw(streams_of[1], (TOKENS, HEADS * HEADDIM), 1.0, 6.0, ((0, 256),)),
        "input_map": bell_draw(streams_of[2], (TOKENS, STATE), (32 * STATE) ** -0.5, 0.09375, ((0, 256),)),
        "output_map": bell_draw(streams_of[3], (TOKENS, STATE), (32 * STATE) ** -0.5, 0.09375, ((0, 256),)),
        "log_decay": draw_log_decay(jax.random.fold_in(streams_of[5], 71), 0),
    }


def mult(form, left, right):
    return jnp.einsum(form, left.astype(jnp.float32), right.astype(jnp.float32), precision=lax.Precision.HIGHEST)


def weigh(values, grads, rates):
    cumulative = jnp.cumsum(rates, axis=1)
    block_decay = cumulative[:, -1]
    decay_tail = jnp.exp(block_decay[:, None] - cumulative)
    decay_lead = jnp.exp(cumulative)
    inputs_tail = (values.astype(jnp.float32) * decay_tail.T[:, :, None]).astype(jnp.bfloat16)
    grads_lead = (grads.astype(jnp.float32) * decay_lead.T[:, :, None]).astype(jnp.bfloat16)
    return cumulative, block_decay, decay_tail, decay_lead, inputs_tail, grads_lead


def block_summary(values, grads, write_map, read_map, rates):
    cumulative, block_decay, decay_tail, decay_lead, inputs_tail, grads_lead = weigh(values, grads, rates)
    own_state = mult('khp,kn->hpn', inputs_tail, write_map)
    own_back = mult('khp,kn->hpn', grads_lead, read_map)
    return block_decay, own_state, own_back


def block_intra(values, grads, write_map, read_map, rates):
    cumulative = jnp.cumsum(rates, axis=1)
    length = rates.shape[1]
    row_ids = lax.broadcasted_iota(jnp.int32, (length, length), 0)
    col_ids = lax.broadcasted_iota(jnp.int32, (length, length), 1)
    causal = (row_ids >= col_ids)[None]
    log_gap = cumulative[:, :, None] - cumulative[:, None, :]
    decay = jnp.where(causal, jnp.exp(jnp.where(causal, log_gap, 0.0)), 0.0)
    scores = jnp.dot(read_map, write_map.T, preferred_element_type=jnp.float32)
    mixing = (scores[None] * decay).astype(jnp.bfloat16)
    y_intra = mult('hij,jhp->ihp', mixing, values)
    dx_intra = mult('hij,ihp->jhp', mixing, grads)
    pair_dots = mult('ihp,jhp->hij', values, grads)
    head_sum = jnp.sum(pair_dots * jnp.swapaxes(decay, 1, 2), axis=0).astype(jnp.bfloat16)
    db_intra = jnp.dot(head_sum, read_map, preferred_element_type=jnp.float32)
    dc_intra = jnp.dot(head_sum.T, write_map, preferred_element_type=jnp.float32)
    return y_intra, dx_intra, db_intra, dc_intra


def block_final(values, grads, write_map, read_map, rates, y_intra, dx_intra, db_intra, dc_intra, state_in, back_in):
    cumulative, block_decay, decay_tail, decay_lead, inputs_tail, grads_lead = weigh(values, grads, rates)
    state_half = state_in.astype(jnp.bfloat16)
    back_half = back_in.astype(jnp.bfloat16)
    outputs_full = y_intra + mult('kn,hpn->khp', read_map, state_half) * decay_lead.T[:, :, None]
    grad_full = dx_intra + mult('kn,hpn->khp', write_map, back_half) * decay_tail.T[:, :, None]
    grad_write = db_intra + mult('khp,hpn->kn', inputs_tail, back_half)
    grad_read = dc_intra + mult('khp,hpn->kn', grads_lead, state_half)
    change = jnp.sum(grads.astype(jnp.float32) * outputs_full - values.astype(jnp.float32) * grad_full, axis=2).T
    return grad_full.astype(jnp.bfloat16), grad_write.astype(jnp.bfloat16), grad_read.astype(jnp.bfloat16), change


def reference(inputs, out_grad, input_map, output_map, log_decay):
    head_count = log_decay.shape[0]
    tokens = inputs.shape[0]
    head_size = inputs.shape[1] // head_count
    blocks = tokens // STRETCH
    parts = (inputs.reshape(blocks, STRETCH, head_count, head_size),
             out_grad.reshape(blocks, STRETCH, head_count, head_size),
             input_map.reshape(blocks, STRETCH, STATE),
             output_map.reshape(blocks, STRETCH, STATE),
             log_decay.reshape(head_count, blocks, STRETCH).transpose(1, 0, 2))
    empty_state = jnp.zeros((head_count, head_size, STATE), jnp.float32)

    def forward(running, pieces):
        block_decay, own_state, own_back = block_summary(*pieces)
        return jnp.exp(block_decay)[:, None, None] * running + own_state, running

    def backward(running, pieces):
        block_decay, own_state, own_back = block_summary(*pieces)
        return jnp.exp(block_decay)[:, None, None] * running + own_back, running

    _, state_stack = lax.scan(forward, empty_state, parts)
    _, back_stack = lax.scan(backward, empty_state, parts, reverse=True)

    def finish(item):
        pieces, state_in, back_in = item
        intra = block_intra(*pieces)
        return block_final(*pieces, *intra, state_in, back_in)

    grad_values, grad_write, grad_read, change = lax.map(finish, (parts, state_stack, back_stack))
    change = change.transpose(1, 0, 2).reshape(head_count, tokens)
    grad_decay = jnp.cumsum(change[:, ::-1], axis=1)[:, ::-1]
    return (grad_values.reshape(tokens, head_count * head_size),
            grad_write.reshape(tokens, STATE),
            grad_read.reshape(tokens, STATE),
            grad_decay)
```

```python
import jax
import jax.numpy as jnp
from jax import lax
from jax.experimental import pallas as pl
from jax.experimental.pallas import tpu as pltpu
from jax.sharding import PartitionSpec as P

MESH = pl.DeviceIdType.MESH
HIGH = lax.Precision.HIGHEST
F32 = jnp.float32
BF16 = jnp.bfloat16
LIMIT = 56 * 2**20

T = 256
HEADS = 40
N = 128
WIDE = 2560
HALF = WIDE // 2
Z, CORES, GROUPS = 8, 2, 16
SLICE = N // Z


def nn(a, b, precision=None):
    return lax.dot_general(
        a, b, (((1,), (0,)), ((), ())), precision=precision, preferred_element_type=F32
    )


def nt(a, b, precision=None):
    return lax.dot_general(
        a, b, (((1,), (1,)), ((), ())), precision=precision, preferred_element_type=F32
    )


def tn(a, b, precision=None):
    return lax.dot_general(
        a, b, (((0,), (0,)), ((), ())), precision=precision, preferred_element_type=F32
    )


def iota(shape, dim):
    return lax.broadcasted_iota(jnp.int32, shape, dim)


def running(rates):
    padded = jnp.concatenate([rates, jnp.zeros((N - HEADS, T), F32)], axis=0)
    upto = (iota((T, T), 1) <= iota((T, T), 0)).astype(F32)
    return padded, nt(upto, padded, HIGH)


def own(v_ref, g_ref, w_ref, r_ref, a_ref, vt_ref, gl_ref, of_ref, ob_ref, log_ref):
    _, cum = running(a_ref[...])
    block = cum[T - 1 : T, :]
    log_ref[...] = jnp.broadcast_to(block, (8, N))
    tail, lead = jnp.exp(block - cum), jnp.exp(cum)
    left = iota((T, N), 1) < N // 2
    w_t, r_t = w_ref[...].T, r_ref[...].T
    for i in range(HEADS // 2):
        at = slice(N * i, N * i + N)
        a, b = 2 * i, 2 * i + 1
        tails = jnp.where(left, tail[:, a : a + 1], tail[:, b : b + 1])
        leads = jnp.where(left, lead[:, a : a + 1], lead[:, b : b + 1])
        vt = (v_ref[:, at].astype(F32) * tails).astype(BF16)
        gl = (g_ref[:, at].astype(F32) * leads).astype(BF16)
        vt_ref[:, at] = vt
        gl_ref[:, at] = gl
        c, lanes = divmod(N * i, HALF)
        of_ref[c, :, lanes : lanes + N] = nn(w_t, vt)
        ob_ref[c, :, lanes : lanes + N] = nn(r_t, gl)


def exchange(
    of, ob, log, sf, sb,
    logs, glogs, xf, xb, cf, cb, uf, ub, pf, pb, tf, tb, df, db, kf, kb, yf, yb,
    wz, ez, fz, ex, wg,
    log_s, log_r, glog_s, glog_r, x_s, x_r, u_s, u_r, t_s, t_r, d_s, d_r,
):
    g, s = lax.axis_index("grp"), lax.axis_index("seq")
    z, c = s // CORES, s % CORES
    other = (g, z * CORES + 1 - c)

    def copy(src, dst, send, recv, device):
        return pltpu.make_async_remote_copy(
            src_ref=src,
            dst_ref=dst,
            send_sem=send,
            recv_sem=recv,
            device_id=device,
            device_id_type=MESH,
        )

    def over(count, mine, step):
        def lap(i, carry):
            step(lax.rem(mine + i, count))
            return carry

        lax.fori_loop(1, count, lap, 0)

    def rows(j):
        return pl.ds(pl.multiple_of(j * SLICE, SLICE), SLICE)

    barrier = pltpu.get_barrier_semaphore()

    def greet(device):
        pl.semaphore_signal(barrier, inc=1, device_id=device, device_id_type=MESH)

    over(Z * CORES, s, lambda k: greet((g, k)))
    over(GROUPS, g, lambda k: greet((k, s)))
    pl.semaphore_wait(barrier, Z * CORES - 1 + GROUPS - 1)

    logs[s] = log[...]

    def log_copy(k):
        return copy(logs.at[s], logs.at[s], log_s.at[k], log_r.at[s], (g, k))

    def log_here(k):
        return copy(logs.at[k], logs.at[k], log_s.at[k], log_r.at[k], (g, k))

    over(Z * CORES, s, lambda k: log_copy(k).start())
    up_f = copy(of.at[1 - c], xf, x_s.at[0], x_r.at[0], other)
    up_b = copy(ob.at[1 - c], xb, x_s.at[1], x_r.at[1], other)
    up_f.start()
    up_b.start()
    over(Z * CORES, s, lambda k: log_here(k).wait_recv())

    blocks = jnp.max(logs[...], axis=1)
    glogs[g] = jnp.broadcast_to(jnp.sum(blocks, axis=0, keepdims=True), (8, N))

    def glog_copy(k):
        return copy(glogs.at[g], glogs.at[g], glog_s.at[k], glog_r.at[g], (k, s))

    def glog_here(k):
        return copy(glogs.at[k], glogs.at[k], glog_s.at[k], glog_r.at[k], (k, s))

    over(GROUPS, g, lambda k: glog_copy(k).start())

    spread = (iota((N, HALF), 0) == iota((N, HALF), 1) // 64 + c * (HEADS // 2)).astype(F32)
    wide = nn(blocks, spread, HIGH)
    chip_of, place = iota((Z, Z * CORES), 1) // CORES, iota((Z, Z * CORES), 0)
    wz[...] = jnp.exp(nn((chip_of == place).astype(F32), wide, HIGH))
    ez[...] = jnp.exp(nn((chip_of < place).astype(F32), wide, HIGH))
    fz[...] = jnp.exp(nn((chip_of > place).astype(F32), wide, HIGH))
    mine = (iota((Z, Z * CORES), 1) == place + z * CORES).astype(F32)
    ex[...] = jnp.exp(nn(mine, wide, HIGH))
    first, second = ex[0:1, :], ex[1:2, :]
    one = jnp.ones_like(first)
    is_first = c == 0

    def slices_up(way, own_ref, theirs, chip, up, a, b):
        def put(j):
            chip[rows(j), :] = a * own_ref[c, rows(j), :] + b * theirs[rows(j), :]

        def send(j):
            put(j)
            copy(chip.at[rows(j)], up.at[z], u_s.at[way, j], u_r.at[way, z], (g, j * CORES + c)).start()

        over(Z, z, send)
        put(z)
        up[z] = chip[rows(z), :]

    up_f.wait_recv()
    slices_up(
        0, of, xf, cf, uf, jnp.where(is_first, second, one), jnp.where(is_first, one, second)
    )
    up_b.wait_recv()
    slices_up(1, ob, xb, cb, ub, jnp.where(is_first, one, first), jnp.where(is_first, first, one))

    def up_here(way, chip, up, j):
        return copy(chip.at[rows(j)], up.at[j], u_s.at[way, j], u_r.at[way, j], (g, j * CORES + c))

    def total_copy(way, total, k):
        return copy(total.at[g], total.at[g], t_s.at[way, k], t_r.at[way, g], (k, s))

    def total_here(way, total, k):
        return copy(total.at[k], total.at[k], t_s.at[way, k], t_r.at[way, k], (k, s))

    def ring(way, chip, up, part, total, order):
        over(Z, z, lambda j: up_here(way, chip, up, j).wait_recv())
        state = jnp.zeros((SLICE, HALF), F32)
        for j in order:
            part[j] = state
            state = wz[j : j + 1, :] * state + up[j]
        total[g] = state
        over(GROUPS, g, lambda k: total_copy(way, total, k).start())

    ring(0, cf, uf, pf, tf, range(Z))
    over(GROUPS, g, lambda k: glog_here(k).wait_recv())
    wg[...] = jnp.exp(nn(jnp.max(glogs[...], axis=1), spread, HIGH))
    ring(1, cb, ub, pb, tb, range(Z - 1, -1, -1))

    def down_copy(way, part, down, j):
        return copy(part.at[j], down.at[rows(z)], d_s.at[way, j], d_r.at[way, z], (g, j * CORES + c))

    def down_here(way, part, down, j):
        return copy(part.at[j], down.at[rows(j)], d_s.at[way, j], d_r.at[way, j], (g, j * CORES + c))

    def groups(way, part, total, down, decay, count, pick):
        over(GROUPS, g, lambda k: total_here(way, total, k).wait_recv())

        def lap(i, state):
            k = pick(i)
            return wg[pl.ds(k, 1), :] * state + total[k]

        state = lax.fori_loop(0, count, lap, jnp.zeros((SLICE, HALF), F32))

        def send(j):
            part[j] += decay[pl.ds(j, 1), :] * state
            down_copy(way, part, down, j).start()

        over(Z, z, send)
        down[rows(z), :] = part[z] + decay[pl.ds(z, 1), :] * state

    groups(0, pf, tf, df, ez, g, lambda i: i)
    groups(1, pb, tb, db, fz, GROUPS - 1 - g, lambda i: GROUPS - 1 - i)

    over(Z, z, lambda j: down_here(0, pf, df, j).wait_recv())
    out_f = copy(kf, yf, x_s.at[2], x_r.at[2], other)

    @pl.when(is_first)
    def _():
        kf[...] = first * df[...] + of[c]
        out_f.start()
        sf[c] = df[...]

    @pl.when(jnp.logical_not(is_first))
    def _():
        kf[...] = df[...]
        out_f.start()
        sf[c] = first * df[...] + xf[...]

    over(Z, z, lambda j: down_here(1, pb, db, j).wait_recv())
    out_b = copy(kb, yb, x_s.at[3], x_r.at[3], other)

    @pl.when(is_first)
    def _():
        kb[...] = db[...]
        out_b.start()
        sb[c] = second * db[...] + xb[...]

    @pl.when(jnp.logical_not(is_first))
    def _():
        kb[...] = second * db[...] + ob[c]
        out_b.start()
        sb[c] = db[...]

    out_f.wait_recv()
    sf[1 - c] = yf[...]
    out_b.wait_recv()
    sb[1 - c] = yb[...]

    over(Z * CORES, s, lambda k: log_copy(k).wait_send())
    over(GROUPS, g, lambda k: glog_copy(k).wait_send())
    for way, chip, up, part, total, down in ((0, cf, uf, pf, tf, df), (1, cb, ub, pb, tb, db)):
        over(Z, z, lambda j: up_here(way, chip, up, j).wait_send())
        over(GROUPS, g, lambda k: total_copy(way, total, k).wait_send())
        over(Z, z, lambda j: down_copy(way, part, down, j).wait_send())
    for each in (up_f, up_b, out_f, out_b):
        each.wait_send()


def finish(
    v_ref, g_ref, w_ref, r_ref, a_ref, vt_ref, gl_ref, of_ref, sf_ref, sb_ref,
    dv_ref, dw_ref, dr_ref, da_ref,
):
    padded, cum = running(a_ref[...])
    upto = (iota((T, T), 0) <= iota((T, T), 1)).astype(F32)
    cum_rows = nn(padded, upto, HIGH)
    block = cum[T - 1 : T, :]
    tail, lead = jnp.exp(block - cum), jnp.exp(cum)
    causal = iota((T, T), 0) >= iota((T, T), 1)
    left = iota((T, N), 1) < N // 2
    left_row = left[0:1, :]
    w, r = w_ref[...], r_ref[...]
    scores = nt(r, w)
    summed = jnp.zeros((T, T), F32)
    change = jnp.zeros((T, N), F32)
    later = jnp.zeros((1, N), F32)
    dw = jnp.zeros((T, N), F32)
    dr = jnp.zeros((T, N), F32)
    bd = jnp.exp(block)
    for i in range(HEADS // 2):
        at = slice(N * i, N * i + N)
        c, lanes = divmod(N * i, HALF)
        within = slice(lanes, lanes + N)
        heads = (2 * i, 2 * i + 1)
        v, g = v_ref[:, at], g_ref[:, at]
        y_two, dx_two = [], []
        for k, h in enumerate(heads):
            gap = cum[:, h : h + 1] - cum_rows[h : h + 1, :]
            decay = jnp.exp(jnp.where(causal, gap, -jnp.inf))
            mixing = (scores * decay).astype(BF16)
            y_two.append(nn(mixing, v))
            dx_two.append(tn(mixing, g))
            one = jnp.where(left if k == 0 else jnp.logical_not(left), g, jnp.zeros_like(g))
            summed = summed + nt(one, v) * decay
        a, b = heads
        tails = jnp.where(left, tail[:, a : a + 1], tail[:, b : b + 1])
        leads = jnp.where(left, lead[:, a : a + 1], lead[:, b : b + 1])
        state, back = sf_ref[c, :, within], sb_ref[c, :, within]
        state_half, back_half = state.astype(BF16), back.astype(BF16)
        y = jnp.where(left, y_two[0], y_two[1]) + nn(r, state_half) * leads
        dx = jnp.where(left, dx_two[0], dx_two[1]) + nn(w, back_half) * tails
        dv_ref[:, at] = dx.astype(BF16)
        dw = dw + nt(vt_ref[:, at], back_half)
        dr = dr + nt(gl_ref[:, at], state_half)
        picks = (iota((N, N), 1) == iota((N, N), 0) // 64 + 2 * i).astype(F32)
        change = change + nn(g.astype(F32) * y - v.astype(F32) * dx, picks, HIGH)
        decays = jnp.where(left_row, bd[:, a : a + 1], bd[:, b : b + 1])
        meet = jnp.sum((decays * state + of_ref[c, :, within]) * back, axis=0, keepdims=True)
        later = later + nn(jnp.broadcast_to(meet, (8, N)), picks, HIGH)[0:1, :]
    half = summed.astype(BF16)
    dw_ref[...] = (dw + tn(half, r)).astype(BF16)
    dr_ref[...] = (dr + nn(half, w)).astype(BF16)
    change = change + jnp.where(iota((T, N), 0) == T - 1, later, 0.0)
    after = (iota((T, T), 0) >= iota((T, T), 1)).astype(F32)
    da_ref[...] = tn(change, after, HIGH)[:HEADS, :]


def vmem(count):
    return [pl.BlockSpec(memory_space=pltpu.VMEM)] * count


def per_device(inputs, out_grad, input_map, output_map, log_decay):
    shape = jax.ShapeDtypeStruct
    states = shape((CORES, N, HALF), F32)
    vt, gl, own_f, own_b, log = pl.pallas_call(
        own,
        out_shape=(shape((T, WIDE), BF16), shape((T, WIDE), BF16), states, states, shape((8, N), F32)),
        in_specs=vmem(5),
        out_specs=tuple(vmem(5)),
        compiler_params=pltpu.CompilerParams(vmem_limit_bytes=LIMIT),
        name="own",
    )(inputs, out_grad, input_map, output_map, log_decay)
    whole = pltpu.VMEM((N, HALF), F32)
    by_z = pltpu.VMEM((Z, SLICE, HALF), F32)
    by_group = pltpu.VMEM((GROUPS, SLICE, HALF), F32)
    dma = pltpu.SemaphoreType.DMA
    state_in, back_in = pl.pallas_call(
        exchange,
        out_shape=(states, states),
        in_specs=vmem(3),
        out_specs=tuple(vmem(2)),
        scratch_shapes=[
            pltpu.VMEM((Z * CORES, 8, N), F32),
            pltpu.VMEM((GROUPS, 8, N), F32),
            *([whole] * 4),
            *([by_z] * 4),
            *([by_group] * 2),
            *([whole] * 6),
            *([pltpu.VMEM((Z, HALF), F32)] * 4),
            pltpu.VMEM((GROUPS, HALF), F32),
            *([dma((GROUPS,))] * 4),
            *([dma((4,))] * 2),
            *([dma((2, Z))] * 2),
            *([dma((2, GROUPS))] * 2),
            *([dma((2, Z))] * 2),
        ],
        compiler_params=pltpu.CompilerParams(
            collective_id=0, has_side_effects=True, vmem_limit_bytes=LIMIT
        ),
        name="exchange",
    )(own_f, own_b, log)
    return pl.pallas_call(
        finish,
        out_shape=(
            shape((T, WIDE), BF16),
            shape((T, N), BF16),
            shape((T, N), BF16),
            shape((HEADS, T), F32),
        ),
        in_specs=vmem(10),
        out_specs=tuple(vmem(4)),
        compiler_params=pltpu.CompilerParams(vmem_limit_bytes=LIMIT),
        name="finish",
    )(inputs, out_grad, input_map, output_map, log_decay, vt, gl, own_f, state_in, back_in)


def solution(mesh):
    tokens = P(("grp", "seq"), None)
    rates = P(None, ("grp", "seq"))
    return jax.shard_map(
        per_device,
        mesh=mesh,
        in_specs=(tokens, tokens, tokens, tokens, rates),
        out_specs=(tokens, tokens, tokens, rates),
        check_vma=False,
    )
```

```python
import jax
import jax.numpy as jnp
from jax import lax
from jax.experimental import pallas as pl
from jax.experimental.pallas import tpu as pltpu
from jax.sharding import PartitionSpec as P

MESH = pl.DeviceIdType.MESH
HIGH = lax.Precision.HIGHEST
F32 = jnp.float32
BF16 = jnp.bfloat16
LIMIT = 56 * 2**20

T = 256
HEADS = 40
N = 128
WIDE = 2560
HALF = WIDE // 2
Z, CORES, GROUPS, SIDE = 8, 2, 16, 4
SLICE = N // Z


def nn(a, b, precision=None):
    return lax.dot_general(
        a, b, (((1,), (0,)), ((), ())), precision=precision, preferred_element_type=F32
    )


def nt(a, b, precision=None):
    return lax.dot_general(
        a, b, (((1,), (1,)), ((), ())), precision=precision, preferred_element_type=F32
    )


def tn(a, b, precision=None):
    return lax.dot_general(
        a, b, (((0,), (0,)), ((), ())), precision=precision, preferred_element_type=F32
    )


def iota(shape, dim):
    return lax.broadcasted_iota(jnp.int32, shape, dim)


def running(rates):
    padded = jnp.concatenate([rates, jnp.zeros((N - HEADS, T), F32)], axis=0)
    upto = (iota((T, T), 1) <= iota((T, T), 0)).astype(F32)
    return padded, nt(upto, padded, HIGH)


def own(v_ref, g_ref, w_ref, r_ref, a_ref, vt_ref, gl_ref, of_ref, ob_ref, log_ref):
    _, cum = running(a_ref[...])
    block = cum[T - 1 : T, :]
    log_ref[...] = jnp.broadcast_to(block, (8, N))
    tail, lead = jnp.exp(block - cum), jnp.exp(cum)
    left = iota((T, N), 1) < N // 2
    w_t, r_t = w_ref[...].T, r_ref[...].T
    for i in range(HEADS // 2):
        at = slice(N * i, N * i + N)
        a, b = 2 * i, 2 * i + 1
        tails = jnp.where(left, tail[:, a : a + 1], tail[:, b : b + 1])
        leads = jnp.where(left, lead[:, a : a + 1], lead[:, b : b + 1])
        vt = (v_ref[:, at].astype(F32) * tails).astype(BF16)
        gl = (g_ref[:, at].astype(F32) * leads).astype(BF16)
        vt_ref[:, at] = vt
        gl_ref[:, at] = gl
        c, lanes = divmod(N * i, HALF)
        of_ref[c, :, lanes : lanes + N] = nn(w_t, vt)
        ob_ref[c, :, lanes : lanes + N] = nn(r_t, gl)


def exchange(
    of, ob, log, sf, sb,
    logs, glogs, xf, xb, cf, cb, uf, ub, pf, pb, tf, tb, rf, rb, df, db, kf, kb, yf, yb,
    wz, ez, fz, ex, wg, wr,
    log_s, log_r, glog_s, glog_r, x_s, x_r, u_s, u_r, t_s, t_r, r_s, r_r, d_s, d_r,
):
    g, s = lax.axis_index("grp"), lax.axis_index("seq")
    z, c = s // CORES, s % CORES
    y, x = g // SIDE, g % SIDE
    partner = z * CORES + 1 - c
    other = (g, partner)

    def copy(src, dst, send, recv, device):
        return pltpu.make_async_remote_copy(
            src_ref=src,
            dst_ref=dst,
            send_sem=send,
            recv_sem=recv,
            device_id=device,
            device_id_type=MESH,
        )

    def over(count, mine, step):
        def lap(i, carry):
            step(lax.rem(mine + i, count))
            return carry

        lax.fori_loop(1, count, lap, 0)

    def rows(j):
        return pl.ds(pl.multiple_of(j * SLICE, SLICE), SLICE)

    barrier = pltpu.get_barrier_semaphore()

    def greet(device):
        pl.semaphore_signal(barrier, inc=1, device_id=device, device_id_type=MESH)

    over(Z * CORES, s, lambda k: greet((g, k)))
    over(GROUPS, g, lambda k: greet((k, s)))
    logs[s] = log[...]
    pl.semaphore_wait(barrier, Z * CORES - 1 + GROUPS - 1)

    def log_copy(k):
        return copy(logs.at[s], logs.at[s], log_s.at[k], log_r.at[s], (g, k))

    def log_here(k):
        return copy(logs.at[k], logs.at[k], log_s.at[k], log_r.at[k], (g, k))

    log_copy(partner).start()
    up_f = copy(of.at[1 - c], xf, x_s.at[0], x_r.at[0], other)
    up_b = copy(ob.at[1 - c], xb, x_s.at[1], x_r.at[1], other)
    up_f.start()
    up_b.start()

    def over_others(step):
        def lap(i, carry):
            step(lax.rem(s - c + CORES + i, Z * CORES))
            return carry

        lax.fori_loop(0, Z * CORES - CORES, lap, 0)

    over_others(lambda k: log_copy(k).start())

    spread = (iota((N, HALF), 0) == iota((N, HALF), 1) // 64 + c * (HEADS // 2)).astype(F32)
    is_first = c == 0
    mine = nn(log[...], spread, HIGH)[0:1, :]
    log_here(partner).wait_recv()
    theirs = nn(logs[partner], spread, HIGH)[0:1, :]
    ex[0:1, :] = jnp.exp(jnp.where(is_first, mine, theirs))
    ex[1:2, :] = jnp.exp(jnp.where(is_first, theirs, mine))
    first, second = ex[0:1, :], ex[1:2, :]
    one = jnp.ones_like(first)

    def slices_up(way, own_ref, theirs, chip, up, a, b):
        def put(j):
            chip[rows(j), :] = a * own_ref[c, rows(j), :] + b * theirs[rows(j), :]

        def send(j):
            put(j)
            copy(chip.at[rows(j)], up.at[z], u_s.at[way, j], u_r.at[way, z], (g, j * CORES + c)).start()

        over(Z, z, send)
        put(z)
        up[z] = chip[rows(z), :]

    up_f.wait_recv()
    slices_up(
        0, of, xf, cf, uf, jnp.where(is_first, second, one), jnp.where(is_first, one, second)
    )
    up_b.wait_recv()
    slices_up(1, ob, xb, cb, ub, jnp.where(is_first, one, first), jnp.where(is_first, first, one))

    over_others(lambda k: log_here(k).wait_recv())
    blocks = jnp.max(logs[...], axis=1)
    glogs[g] = jnp.broadcast_to(jnp.sum(blocks, axis=0, keepdims=True), (8, N))

    def glog_copy(k):
        return copy(glogs.at[g], glogs.at[g], glog_s.at[k], glog_r.at[g], (k, s))

    def glog_here(k):
        return copy(glogs.at[k], glogs.at[k], glog_s.at[k], glog_r.at[k], (k, s))

    over(GROUPS, g, lambda k: glog_copy(k).start())
    wide = nn(blocks, spread, HIGH)
    chip_of, place = iota((Z, Z * CORES), 1) // CORES, iota((Z, Z * CORES), 0)
    wz[...] = jnp.exp(nn((chip_of == place).astype(F32), wide, HIGH))
    ez[...] = jnp.exp(nn((chip_of < place).astype(F32), wide, HIGH))
    fz[...] = jnp.exp(nn((chip_of > place).astype(F32), wide, HIGH))
    over(GROUPS, g, lambda k: glog_here(k).wait_recv())
    wide = nn(jnp.max(glogs[...], axis=1), spread, HIGH)
    wg[...] = jnp.exp(wide)
    row_of, column_of = iota((8, GROUPS), 1) // SIDE, iota((8, GROUPS), 1) % SIDE
    place = iota((8, GROUPS), 0)
    beside = ((place == SIDE) & (column_of < x)) | ((place == SIDE + 1) & (column_of > x))
    picks = ((place < SIDE) & (row_of == place)) | ((row_of == y) & beside)
    wr[...] = jnp.exp(nn(picks.astype(F32), wide, HIGH))

    def up_here(way, chip, up, j):
        return copy(chip.at[rows(j)], up.at[j], u_s.at[way, j], u_r.at[way, j], (g, j * CORES + c))

    def total_copy(way, total, k):
        return copy(total.at[x], total.at[x], t_s.at[way, k], t_r.at[way, x], (y * SIDE + k, s))

    def total_here(way, total, k):
        return copy(total.at[k], total.at[k], t_s.at[way, k], t_r.at[way, k], (y * SIDE + k, s))

    def row_copy(way, total, k):
        return copy(total.at[y], total.at[y], r_s.at[way, k], r_r.at[way, y], (k * SIDE + x, s))

    def row_here(way, total, k):
        return copy(total.at[k], total.at[k], r_s.at[way, k], r_r.at[way, k], (k * SIDE + x, s))

    def down_copy(way, part, down, j):
        return copy(part.at[j], down.at[rows(z)], d_s.at[way, j], d_r.at[way, z], (g, j * CORES + c))

    def down_here(way, part, down, j):
        return copy(part.at[j], down.at[rows(j)], d_s.at[way, j], d_r.at[way, j], (g, j * CORES + c))

    empty = jnp.zeros((SLICE, HALF), F32)

    def ring(way, chip, up, part, total, order):
        over(Z, z, lambda j: up_here(way, chip, up, j).wait_recv())
        state = empty
        for j in order:
            part[j] = state
            state = wz[j : j + 1, :] * state + up[j]
        total[x] = state
        over(SIDE, x, lambda k: total_copy(way, total, k).start())

    def row(way, total, row_total, order):
        over(SIDE, x, lambda k: total_here(way, total, k).wait_recv())
        state, before = empty, empty
        for k in order:
            before = jnp.where(k == x, state, before)
            state = wg[pl.ds(y * SIDE + k, 1), :] * state + total[k]
        row_total[y] = state
        over(SIDE, y, lambda k: row_copy(way, row_total, k).start())
        total[SIDE] = before

    def column(way, part, total, row_total, down, decay, order):
        over(SIDE, y, lambda k: row_here(way, row_total, k).wait_recv())
        state, before = empty, empty
        for k in order:
            before = jnp.where(k == y, state, before)
            state = wr[k : k + 1, :] * state + row_total[k]
        state = wr[SIDE + way : SIDE + way + 1, :] * before + total[SIDE]

        def send(j):
            part[j] += decay[pl.ds(j, 1), :] * state
            down_copy(way, part, down, j).start()

        over(Z, z, send)
        down[rows(z), :] = part[z] + decay[pl.ds(z, 1), :] * state

    ahead, back = range(SIDE), range(SIDE - 1, -1, -1)
    ring(0, cf, uf, pf, tf, range(Z))
    row(0, tf, rf, ahead)
    ring(1, cb, ub, pb, tb, range(Z - 1, -1, -1))
    column(0, pf, tf, rf, df, ez, ahead)
    row(1, tb, rb, back)
    column(1, pb, tb, rb, db, fz, back)

    over(Z, z, lambda j: down_here(0, pf, df, j).wait_recv())
    out_f = copy(kf, yf, x_s.at[2], x_r.at[2], other)

    @pl.when(is_first)
    def _():
        kf[...] = first * df[...] + of[c]
        out_f.start()
        sf[c] = df[...]

    @pl.when(jnp.logical_not(is_first))
    def _():
        kf[...] = df[...]
        out_f.start()
        sf[c] = first * df[...] + xf[...]

    over(Z, z, lambda j: down_here(1, pb, db, j).wait_recv())
    out_b = copy(kb, yb, x_s.at[3], x_r.at[3], other)

    @pl.when(is_first)
    def _():
        kb[...] = db[...]
        out_b.start()
        sb[c] = second * db[...] + xb[...]

    @pl.when(jnp.logical_not(is_first))
    def _():
        kb[...] = second * db[...] + ob[c]
        out_b.start()
        sb[c] = db[...]

    out_f.wait_recv()
    sf[1 - c] = yf[...]
    out_b.wait_recv()
    sb[1 - c] = yb[...]

    over(Z * CORES, s, lambda k: log_copy(k).wait_send())
    over(GROUPS, g, lambda k: glog_copy(k).wait_send())
    for way, chip, up, part, total, row_total, down in (
        (0, cf, uf, pf, tf, rf, df),
        (1, cb, ub, pb, tb, rb, db),
    ):
        over(Z, z, lambda j: up_here(way, chip, up, j).wait_send())
        over(SIDE, x, lambda k: total_copy(way, total, k).wait_send())
        over(SIDE, y, lambda k: row_copy(way, row_total, k).wait_send())
        over(Z, z, lambda j: down_copy(way, part, down, j).wait_send())
    for each in (up_f, up_b, out_f, out_b):
        each.wait_send()


def finish(
    v_ref, g_ref, w_ref, r_ref, a_ref, vt_ref, gl_ref, of_ref, sf_ref, sb_ref,
    dv_ref, dw_ref, dr_ref, da_ref,
):
    padded, cum = running(a_ref[...])
    upto = (iota((T, T), 0) <= iota((T, T), 1)).astype(F32)
    cum_rows = nn(padded, upto, HIGH)
    block = cum[T - 1 : T, :]
    tail, lead = jnp.exp(block - cum), jnp.exp(cum)
    causal = iota((T, T), 0) >= iota((T, T), 1)
    left = iota((T, N), 1) < N // 2
    left_row = left[0:1, :]
    w, r = w_ref[...], r_ref[...]
    scores = nt(r, w)
    summed = jnp.zeros((T, T), F32)
    change = jnp.zeros((T, N), F32)
    later = jnp.zeros((1, N), F32)
    dw = jnp.zeros((T, N), F32)
    dr = jnp.zeros((T, N), F32)
    bd = jnp.exp(block)
    for i in range(HEADS // 2):
        at = slice(N * i, N * i + N)
        c, lanes = divmod(N * i, HALF)
        within = slice(lanes, lanes + N)
        heads = (2 * i, 2 * i + 1)
        v, g = v_ref[:, at], g_ref[:, at]
        y_two, dx_two = [], []
        for k, h in enumerate(heads):
            gap = cum[:, h : h + 1] - cum_rows[h : h + 1, :]
            decay = jnp.exp(jnp.where(causal, gap, -jnp.inf))
            mixing = (scores * decay).astype(BF16)
            y_two.append(nn(mixing, v))
            dx_two.append(tn(mixing, g))
            one = jnp.where(left if k == 0 else jnp.logical_not(left), g, jnp.zeros_like(g))
            summed = summed + nt(one, v) * decay
        a, b = heads
        tails = jnp.where(left, tail[:, a : a + 1], tail[:, b : b + 1])
        leads = jnp.where(left, lead[:, a : a + 1], lead[:, b : b + 1])
        state, back = sf_ref[c, :, within], sb_ref[c, :, within]
        state_half, back_half = state.astype(BF16), back.astype(BF16)
        y = jnp.where(left, y_two[0], y_two[1]) + nn(r, state_half) * leads
        dx = jnp.where(left, dx_two[0], dx_two[1]) + nn(w, back_half) * tails
        dv_ref[:, at] = dx.astype(BF16)
        dw = dw + nt(vt_ref[:, at], back_half)
        dr = dr + nt(gl_ref[:, at], state_half)
        picks = (iota((N, N), 1) == iota((N, N), 0) // 64 + 2 * i).astype(F32)
        change = change + nn(g.astype(F32) * y - v.astype(F32) * dx, picks, HIGH)
        decays = jnp.where(left_row, bd[:, a : a + 1], bd[:, b : b + 1])
        meet = jnp.sum((decays * state + of_ref[c, :, within]) * back, axis=0, keepdims=True)
        later = later + nn(jnp.broadcast_to(meet, (8, N)), picks, HIGH)[0:1, :]
    half = summed.astype(BF16)
    dw_ref[...] = (dw + tn(half, r)).astype(BF16)
    dr_ref[...] = (dr + nn(half, w)).astype(BF16)
    change = change + jnp.where(iota((T, N), 0) == T - 1, later, 0.0)
    after = (iota((T, T), 0) >= iota((T, T), 1)).astype(F32)
    da_ref[...] = tn(change, after, HIGH)[:HEADS, :]


def vmem(count):
    return [pl.BlockSpec(memory_space=pltpu.VMEM)] * count


def per_device(inputs, out_grad, input_map, output_map, log_decay):
    shape = jax.ShapeDtypeStruct
    states = shape((CORES, N, HALF), F32)
    vt, gl, own_f, own_b, log = pl.pallas_call(
        own,
        out_shape=(shape((T, WIDE), BF16), shape((T, WIDE), BF16), states, states, shape((8, N), F32)),
        in_specs=vmem(5),
        out_specs=tuple(vmem(5)),
        compiler_params=pltpu.CompilerParams(vmem_limit_bytes=LIMIT),
        name="own",
    )(inputs, out_grad, input_map, output_map, log_decay)
    whole = pltpu.VMEM((N, HALF), F32)
    by_z = pltpu.VMEM((Z, SLICE, HALF), F32)
    by_side = pltpu.VMEM((SIDE + 1, SLICE, HALF), F32)
    dma = pltpu.SemaphoreType.DMA
    state_in, back_in = pl.pallas_call(
        exchange,
        out_shape=(states, states),
        in_specs=vmem(3),
        out_specs=tuple(vmem(2)),
        scratch_shapes=[
            pltpu.VMEM((Z * CORES, 8, N), F32),
            pltpu.VMEM((GROUPS, 8, N), F32),
            *([whole] * 4),
            *([by_z] * 4),
            *([by_side] * 4),
            *([whole] * 6),
            *([pltpu.VMEM((Z, HALF), F32)] * 4),
            pltpu.VMEM((GROUPS, HALF), F32),
            pltpu.VMEM((8, HALF), F32),
            *([dma((GROUPS,))] * 4),
            *([dma((4,))] * 2),
            *([dma((2, Z))] * 2),
            *([dma((2, SIDE))] * 4),
            *([dma((2, Z))] * 2),
        ],
        compiler_params=pltpu.CompilerParams(
            collective_id=0, has_side_effects=True, vmem_limit_bytes=LIMIT
        ),
        name="exchange",
    )(own_f, own_b, log)
    return pl.pallas_call(
        finish,
        out_shape=(
            shape((T, WIDE), BF16),
            shape((T, N), BF16),
            shape((T, N), BF16),
            shape((HEADS, T), F32),
        ),
        in_specs=vmem(10),
        out_specs=tuple(vmem(4)),
        compiler_params=pltpu.CompilerParams(vmem_limit_bytes=LIMIT),
        name="finish",
    )(inputs, out_grad, input_map, output_map, log_decay, vt, gl, own_f, state_in, back_in)


def solution(mesh):
    tokens = P(("grp", "seq"), None)
    rates = P(None, ("grp", "seq"))
    return jax.shard_map(
        per_device,
        mesh=mesh,
        in_specs=(tokens, tokens, tokens, tokens, rates),
        out_specs=(tokens, tokens, tokens, rates),
        check_vma=False,
    )
```

```python
import jax
import jax.numpy as jnp
from jax import lax
from jax.experimental import pallas as pl
from jax.experimental.pallas import tpu as pltpu
from jax.sharding import PartitionSpec as P

MESH = pl.DeviceIdType.MESH
HIGH = lax.Precision.HIGHEST
F32 = jnp.float32
BF16 = jnp.bfloat16
LIMIT = 56 * 2**20

T = 256
HEADS = 40
N = 128
WIDE = 2560
HALF = WIDE // 2
Z, CORES, GROUPS, SIDE = 8, 2, 16, 4
SLICE = N // Z
PIECES = 4
CHUNK = 256
CUTS = (14, 16, 18)


def nn(a, b, precision=None):
    return lax.dot_general(
        a, b, (((1,), (0,)), ((), ())), precision=precision, preferred_element_type=F32
    )


def nt(a, b, precision=None):
    return lax.dot_general(
        a, b, (((1,), (1,)), ((), ())), precision=precision, preferred_element_type=F32
    )


def tn(a, b, precision=None):
    return lax.dot_general(
        a, b, (((0,), (0,)), ((), ())), precision=precision, preferred_element_type=F32
    )


def iota(shape, dim):
    return lax.broadcasted_iota(jnp.int32, shape, dim)


def block(
    v_ref, g_ref, w_ref, r_ref, a_ref, dv_ref, dw_ref, dr_ref, da_ref,
    cr, cx, vt, gl, of, ob, yi, di, sm, dw, dr, ch,
    logs, glogs, xf, xb, cf, cb, uf, ub, pf, pb, tf, tb, rf, rb, df, db, kf, kb, sf, sb,
    wz, ez, fz, ex, wg, wr,
    log_s, log_r, glog_s, glog_r, x_s, x_r, u_s, u_r, t_s, t_r, r_s, r_r, d_s, d_r,
):
    g, s = lax.axis_index("grp"), lax.axis_index("seq")
    z, c = s // CORES, s % CORES
    y, x = g // SIDE, g % SIDE
    partner = z * CORES + 1 - c
    other = (g, partner)

    def copy(src, dst, send, recv, device):
        return pltpu.make_async_remote_copy(
            src_ref=src,
            dst_ref=dst,
            send_sem=send,
            recv_sem=recv,
            device_id=device,
            device_id_type=MESH,
        )

    def loop(first, last, step):
        def lap(i, carry):
            step(i)
            return carry

        lax.fori_loop(first, last, lap, 0)

    def over(count, mine, step):
        loop(1, count, lambda i: step(lax.rem(mine + i, count)))

    def over_others(step):
        loop(0, Z * CORES - CORES, lambda i: step(lax.rem(s - c + CORES + i, Z * CORES)))

    def rows(j):
        return pl.ds(pl.multiple_of(j * SLICE, SLICE), SLICE)

    def lanes(start, size):
        return pl.ds(pl.multiple_of(start, N), size)

    barrier = pltpu.get_barrier_semaphore()

    def greet(device):
        pl.semaphore_signal(barrier, inc=1, device_id=device, device_id_type=MESH)

    over(Z * CORES, s, lambda k: greet((g, k)))
    over(GROUPS, g, lambda k: greet((k, s)))

    padded = jnp.concatenate([a_ref[...], jnp.zeros((N - HEADS, T), F32)], axis=0)
    upto = (iota((T, T), 0) <= iota((T, T), 1)).astype(F32)
    cum_rows = nn(padded, upto, HIGH)
    cr[...] = cum_rows
    cum = cum_rows.T
    log = jnp.broadcast_to(cum[T - 1 : T, :], (8, N))
    logs[s] = log
    pl.semaphore_wait(barrier, Z * CORES - 1 + GROUPS - 1)

    def log_copy(k):
        return copy(logs.at[s], logs.at[s], log_s.at[k], log_r.at[s], (g, k))

    def log_here(k):
        return copy(logs.at[k], logs.at[k], log_s.at[k], log_r.at[k], (g, k))

    log_copy(partner).start()
    over_others(lambda k: log_copy(k).start())
    left = iota((T, N), 1) < N // 2
    for i in range(HEADS // 2):
        cx[:, N * i : N * i + N] = jnp.where(left, cum[:, 2 * i : 2 * i + 1], cum[:, 2 * i + 1 : 2 * i + 2])

    def own(half, map_t, token_ref, weighted, state, weight):
        def step(k):
            at = lanes(half * HALF + k * CHUNK, CHUNK)
            part = (token_ref[:, at].astype(F32) * weight(at)).astype(BF16)
            weighted[:, at] = part
            state[half, :, lanes(k * CHUNK, CHUNK)] = nn(map_t, part)

        loop(0, HALF // CHUNK, step)

    def tails(at):
        return jnp.exp(cx[T - 1 : T, at] - cx[:, at])

    def leads(at):
        return jnp.exp(cx[:, at])

    w, r = w_ref[...], r_ref[...]
    w_t, r_t = w.T, r.T
    up_f = copy(of.at[1 - c], xf, x_s.at[0], x_r.at[0], other)
    up_b = copy(ob.at[1 - c], xb, x_s.at[1], x_r.at[1], other)
    own(1 - c, w_t, v_ref, vt, of, tails)
    up_f.start()
    own(c, w_t, v_ref, vt, of, tails)

    spread = (iota((N, HALF), 0) == iota((N, HALF), 1) // 64 + c * (HEADS // 2)).astype(F32)
    is_first = c == 0
    mine = nn(log, spread, HIGH)[0:1, :]
    log_here(partner).wait_recv()
    theirs = nn(logs[partner], spread, HIGH)[0:1, :]
    ex[0:1, :] = jnp.exp(jnp.where(is_first, mine, theirs))
    ex[1:2, :] = jnp.exp(jnp.where(is_first, theirs, mine))
    first, second = ex[0:1, :], ex[1:2, :]
    one = jnp.ones_like(first)

    def slices_up(way, own_ref, theirs, chip, up, a, b):
        def put(j):
            chip[rows(j), :] = a * own_ref[c, rows(j), :] + b * theirs[rows(j), :]

        def send(j):
            put(j)
            copy(chip.at[rows(j)], up.at[z], u_s.at[way, j], u_r.at[way, z], (g, j * CORES + c)).start()

        over(Z, z, send)
        put(z)
        up[z] = chip[rows(z), :]

    up_f.wait_recv()
    slices_up(
        0, of, xf, cf, uf, jnp.where(is_first, second, one), jnp.where(is_first, one, second)
    )

    own(1 - c, r_t, g_ref, gl, ob, leads)
    up_b.start()
    own(c, r_t, g_ref, gl, ob, leads)

    def glog_copy(k):
        return copy(glogs.at[g], glogs.at[g], glog_s.at[k], glog_r.at[g], (k, s))

    def glog_here(k):
        return copy(glogs.at[k], glogs.at[k], glog_s.at[k], glog_r.at[k], (k, s))

    over_others(lambda k: log_here(k).wait_recv())
    blocks = jnp.max(logs[...], axis=1)
    glogs[g] = jnp.broadcast_to(jnp.sum(blocks, axis=0, keepdims=True), (8, N))
    over(GROUPS, g, lambda k: glog_copy(k).start())

    up_b.wait_recv()
    slices_up(1, ob, xb, cb, ub, jnp.where(is_first, one, first), jnp.where(is_first, first, one))

    wide = nn(blocks, spread, HIGH)
    chip_of, place = iota((Z, Z * CORES), 1) // CORES, iota((Z, Z * CORES), 0)
    wz[...] = jnp.exp(nn((chip_of == place).astype(F32), wide, HIGH))
    ez[...] = jnp.exp(nn((chip_of < place).astype(F32), wide, HIGH))
    fz[...] = jnp.exp(nn((chip_of > place).astype(F32), wide, HIGH))
    over(GROUPS, g, lambda k: glog_here(k).wait_recv())
    wide = nn(jnp.max(glogs[...], axis=1), spread, HIGH)
    wg[...] = jnp.exp(wide)
    row_of, column_of = iota((8, GROUPS), 1) // SIDE, iota((8, GROUPS), 1) % SIDE
    place = iota((8, GROUPS), 0)
    beside = ((place == SIDE) & (column_of < x)) | ((place == SIDE + 1) & (column_of > x))
    picks = ((place < SIDE) & (row_of == place)) | ((row_of == y) & beside)
    wr[...] = jnp.exp(nn(picks.astype(F32), wide, HIGH))

    causal = iota((T, T), 0) >= iota((T, T), 1)
    scores = nt(r, w)
    sm[...] = jnp.zeros((T, T), F32)

    def intra(i):
        at = lanes(i * N, N)
        v, gr, two = v_ref[:, at], g_ref[:, at], cx[:, at]
        y_two, dx_two = [], []
        total = sm[...]
        for k in range(2):
            gap = two[:, 64 * k : 64 * k + 1] - cr[pl.ds(2 * i + k, 1), :]
            decay = jnp.exp(jnp.where(causal, gap, -jnp.inf))
            mixing = (scores * decay).astype(BF16)
            y_two.append(nn(mixing, v))
            dx_two.append(tn(mixing, gr))
            head = jnp.where(left if k == 0 else jnp.logical_not(left), gr, jnp.zeros_like(gr))
            total = total + nt(head, v) * decay
        sm[...] = total
        yi[:, at] = jnp.where(left, y_two[0], y_two[1])
        di[:, at] = jnp.where(left, dx_two[0], dx_two[1])

    loop(0, CUTS[0], intra)

    def up_here(way, chip, up, j):
        return copy(chip.at[rows(j)], up.at[j], u_s.at[way, j], u_r.at[way, j], (g, j * CORES + c))

    def total_copy(way, total, k):
        return copy(total.at[x], total.at[x], t_s.at[way, k], t_r.at[way, x], (y * SIDE + k, s))

    def total_here(way, total, k):
        return copy(total.at[k], total.at[k], t_s.at[way, k], t_r.at[way, k], (y * SIDE + k, s))

    def row_copy(way, total, k):
        return copy(total.at[y], total.at[y], r_s.at[way, k], r_r.at[way, y], (k * SIDE + x, s))

    def row_here(way, total, k):
        return copy(total.at[k], total.at[k], r_s.at[way, k], r_r.at[way, k], (k * SIDE + x, s))

    def down_copy(way, part, down, j):
        return copy(part.at[j], down.at[rows(z)], d_s.at[way, j], d_r.at[way, z], (g, j * CORES + c))

    def down_here(way, part, down, j):
        return copy(part.at[j], down.at[rows(j)], d_s.at[way, j], d_r.at[way, j], (g, j * CORES + c))

    empty = jnp.zeros((SLICE, HALF), F32)

    def ring(way, chip, up, part, total, order):
        over(Z, z, lambda j: up_here(way, chip, up, j).wait_recv())
        state = empty
        for j in order:
            part[j] = state
            state = wz[j : j + 1, :] * state + up[j]
        total[x] = state
        over(SIDE, x, lambda k: total_copy(way, total, k).start())

    def row(way, total, row_total, order):
        over(SIDE, x, lambda k: total_here(way, total, k).wait_recv())
        state, before = empty, empty
        for k in order:
            before = jnp.where(k == x, state, before)
            state = wg[pl.ds(y * SIDE + k, 1), :] * state + total[k]
        row_total[y] = state
        over(SIDE, y, lambda k: row_copy(way, row_total, k).start())
        total[SIDE] = before

    def column(way, part, total, row_total, down, decay, order):
        over(SIDE, y, lambda k: row_here(way, row_total, k).wait_recv())
        state, before = empty, empty
        for k in order:
            before = jnp.where(k == y, state, before)
            state = wr[k : k + 1, :] * state + row_total[k]
        state = wr[SIDE + way : SIDE + way + 1, :] * before + total[SIDE]

        def send(j):
            part[j] += decay[pl.ds(j, 1), :] * state
            down_copy(way, part, down, j).start()

        over(Z, z, send)
        down[rows(z), :] = part[z] + decay[pl.ds(z, 1), :] * state

    ahead, back = range(SIDE), range(SIDE - 1, -1, -1)
    ring(0, cf, uf, pf, tf, range(Z))
    loop(CUTS[0], CUTS[1], intra)
    row(0, tf, rf, ahead)
    loop(CUTS[1], CUTS[2], intra)
    ring(1, cb, ub, pb, tb, range(Z - 1, -1, -1))
    column(0, pf, tf, rf, df, ez, ahead)
    loop(CUTS[2], HEADS // 2, intra)
    row(1, tb, rb, back)
    half = sm[...].astype(BF16)
    dw[...] = tn(half, r)
    dr[...] = nn(half, w)
    column(1, pb, tb, rb, db, fz, back)

    def finish_f(side):
        def step(k):
            at, within = lanes(side * HALF + k * CHUNK, CHUNK), lanes(k * CHUNK, CHUNK)
            state = sf[side, :, within]
            state_half = state.astype(BF16)
            full = yi[:, at] + nn(r, state_half) * leads(at)
            yi[:, at] = g_ref[:, at].astype(F32) * full
            dr[...] += nt(gl[:, at], state_half)
            sf[side, :, within] = jnp.exp(cx[T - 1 : T, at]) * state + of[side, :, within]

        loop(0, HALF // CHUNK, step)

    last = iota((T, CHUNK), 0) == T - 1
    ch[...] = jnp.zeros((T, N), F32)

    def finish_b(side):
        def step(k):
            at, within = lanes(side * HALF + k * CHUNK, CHUNK), lanes(k * CHUNK, CHUNK)
            back_in = sb[side, :, within]
            back_half = back_in.astype(BF16)
            full = di[:, at] + nn(w, back_half) * tails(at)
            dv_ref[:, at] = full.astype(BF16)
            dw[...] += nt(vt[:, at], back_half)
            meet = jnp.sum(sf[side, :, within] * back_in, axis=0, keepdims=True)
            change = yi[:, at] - v_ref[:, at].astype(F32) * full + jnp.where(last, meet, 0.0)
            high = change.astype(BF16)
            low = (change - high.astype(F32)).astype(BF16)
            head = (side * HALF + k * CHUNK) // 64 + iota((CHUNK, N), 0) // 64
            picks = (iota((CHUNK, N), 1) == head).astype(F32).astype(BF16)
            ch[...] += nn(high, picks) + nn(low, picks)

        loop(0, HALF // CHUNK, step)

    over(Z, z, lambda j: down_here(0, pf, df, j).wait_recv())
    out_f = copy(kf, sf.at[c], x_s.at[2], x_r.at[2], other)

    @pl.when(is_first)
    def _():
        kf[...] = first * df[...] + of[c]
        sf[c] = df[...]

    @pl.when(jnp.logical_not(is_first))
    def _():
        kf[...] = df[...]
        sf[c] = first * df[...] + xf[...]

    out_f.start()
    finish_f(c)
    out_f.wait_recv()
    finish_f(1 - c)

    over(Z, z, lambda j: down_here(1, pb, db, j).wait_recv())
    out_b = copy(kb, sb.at[c], x_s.at[3], x_r.at[3], other)

    @pl.when(is_first)
    def _():
        kb[...] = db[...]
        sb[c] = second * db[...] + xb[...]

    @pl.when(jnp.logical_not(is_first))
    def _():
        kb[...] = second * db[...] + ob[c]
        sb[c] = db[...]

    out_b.start()
    finish_b(c)
    out_b.wait_recv()
    finish_b(1 - c)
    dw_ref[...] = dw[...].astype(BF16)
    dr_ref[...] = dr[...].astype(BF16)
    after = (iota((T, T), 0) >= iota((T, T), 1)).astype(F32)
    da_ref[...] = tn(ch[...], after, HIGH)[:HEADS, :]

    over(Z * CORES, s, lambda k: log_copy(k).wait_send())
    over(GROUPS, g, lambda k: glog_copy(k).wait_send())
    for way, chip, up, part, total, row_total, down in (
        (0, cf, uf, pf, tf, rf, df),
        (1, cb, ub, pb, tb, rb, db),
    ):
        over(Z, z, lambda j: up_here(way, chip, up, j).wait_send())
        over(SIDE, x, lambda k: total_copy(way, total, k).wait_send())
        over(SIDE, y, lambda k: row_copy(way, row_total, k).wait_send())
        over(Z, z, lambda j: down_copy(way, part, down, j).wait_send())
    for each in (up_f, up_b, out_f, out_b):
        each.wait_send()


def deliver(dv_in, dw_in, dr_in, da_in, dv_ref, dw_ref, dr_ref, da_ref, dv, dw, dr, da, sem):
    step = T // PIECES
    pieces = [pl.ds(i * step, step) for i in range(PIECES)]
    ways = [(dv_in.at[at], dv.at[at], dv_ref.at[at]) for at in pieces]
    ways += [(dw_in, dw, dw_ref), (dr_in, dr, dr_ref), (da_in, da, da_ref)]
    inward = [pltpu.make_async_copy(a, b, sem.at[0, i]) for i, (a, b, _) in enumerate(ways)]
    outward = [pltpu.make_async_copy(b, c, sem.at[1, i]) for i, (_, b, c) in enumerate(ways)]
    for each in inward:
        each.start()
    for one, two in zip(inward, outward):
        one.wait()
        two.start()
    for each in outward:
        each.wait()


def vmem(count):
    return [pl.BlockSpec(memory_space=pltpu.VMEM)] * count


def per_device(inputs, out_grad, input_map, output_map, log_decay):
    shape = jax.ShapeDtypeStruct
    whole = pltpu.VMEM((N, HALF), F32)
    both = pltpu.VMEM((CORES, N, HALF), F32)
    by_z = pltpu.VMEM((Z, SLICE, HALF), F32)
    by_side = pltpu.VMEM((SIDE + 1, SLICE, HALF), F32)
    dma = pltpu.SemaphoreType.DMA
    outs = (
        shape((T, WIDE), BF16),
        shape((T, N), BF16),
        shape((T, N), BF16),
        shape((HEADS, T), F32),
    )
    made = pl.pallas_call(
        block,
        out_shape=outs,
        in_specs=vmem(5),
        out_specs=tuple(vmem(4)),
        scratch_shapes=[
            pltpu.VMEM((N, T), F32),
            pltpu.VMEM((T, WIDE), F32),
            *([pltpu.VMEM((T, WIDE), BF16)] * 2),
            *([both] * 2),
            *([pltpu.VMEM((T, WIDE), F32)] * 2),
            pltpu.VMEM((T, T), F32),
            *([pltpu.VMEM((T, N), F32)] * 3),
            pltpu.VMEM((Z * CORES, 8, N), F32),
            pltpu.VMEM((GROUPS, 8, N), F32),
            *([whole] * 4),
            *([by_z] * 4),
            *([by_side] * 4),
            *([whole] * 4),
            *([both] * 2),
            *([pltpu.VMEM((Z, HALF), F32)] * 4),
            pltpu.VMEM((GROUPS, HALF), F32),
            pltpu.VMEM((8, HALF), F32),
            *([dma((GROUPS,))] * 4),
            *([dma((4,))] * 2),
            *([dma((2, Z))] * 2),
            *([dma((2, SIDE))] * 4),
            *([dma((2, Z))] * 2),
        ],
        compiler_params=pltpu.CompilerParams(
            collective_id=0, has_side_effects=True, vmem_limit_bytes=LIMIT
        ),
        name="block",
    )(inputs, out_grad, input_map, output_map, log_decay)
    anywhere = [pl.BlockSpec(memory_space=pl.ANY)] * 4
    return pl.pallas_call(
        deliver,
        out_shape=outs,
        in_specs=anywhere,
        out_specs=tuple(anywhere),
        scratch_shapes=[*(pltpu.VMEM(o.shape, o.dtype) for o in outs), dma((2, PIECES + 3))],
        compiler_params=pltpu.CompilerParams(vmem_limit_bytes=LIMIT),
        name="deliver",
    )(*made)


def solution(mesh):
    tokens = P(("grp", "seq"), None)
    rates = P(None, ("grp", "seq"))
    return jax.shard_map(
        per_device,
        mesh=mesh,
        in_specs=(tokens, tokens, tokens, tokens, rates),
        out_specs=(tokens, tokens, tokens, rates),
        check_vma=False,
    )
```

```python
import jax
import jax.numpy as jnp
from jax import lax
from jax.experimental import pallas as pl
from jax.experimental.pallas import tpu as pltpu
from jax.sharding import PartitionSpec as P

MESH = pl.DeviceIdType.MESH
HIGH = lax.Precision.HIGHEST
F32 = jnp.float32
BF16 = jnp.bfloat16
LIMIT = 56 * 2**20

T = 256
HEADS = 40
N = 128
WIDE = 2560
HALF = WIDE // 2
Z, CORES, GROUPS, SIDE = 8, 2, 16, 4
SLICE = N // Z
PIECES = 4
CHUNK = 256
CUTS = (14, 16, 18)


def nn(a, b, precision=None):
    return lax.dot_general(
        a, b, (((1,), (0,)), ((), ())), precision=precision, preferred_element_type=F32
    )


def nt(a, b, precision=None):
    return lax.dot_general(
        a, b, (((1,), (1,)), ((), ())), precision=precision, preferred_element_type=F32
    )


def tn(a, b, precision=None):
    return lax.dot_general(
        a, b, (((0,), (0,)), ((), ())), precision=precision, preferred_element_type=F32
    )


def iota(shape, dim):
    return lax.broadcasted_iota(jnp.int32, shape, dim)


def block(
    v_ref, g_ref, w_ref, r_ref, a_ref, dv_ref, dw_ref, dr_ref, da_ref,
    cr, cx, vt, gl, of, ob, yi, di, sm, dw, dr, ch,
    logs, glogs, xf, xb, cf, cb, uf, ub, pf, pb, tf, tb, rf, rb, df, db, kf, kb, sf, sb,
    wz, ez, fz, ex, wg, wr,
    log_s, log_r, glog_s, glog_r, x_s, x_r, h_s, h_r, u_s, u_r, t_s, t_r, r_s, r_r, d_s, d_r,
):
    g, s = lax.axis_index("grp"), lax.axis_index("seq")
    z, c = s // CORES, s % CORES
    y, x = g // SIDE, g % SIDE
    partner = z * CORES + 1 - c
    other = (g, partner)

    def copy(src, dst, send, recv, device):
        return pltpu.make_async_remote_copy(
            src_ref=src,
            dst_ref=dst,
            send_sem=send,
            recv_sem=recv,
            device_id=device,
            device_id_type=MESH,
        )

    def loop(first, last, step):
        def lap(i, carry):
            step(i)
            return carry

        lax.fori_loop(first, last, lap, 0)

    def over(count, mine, step):
        loop(1, count, lambda i: step(lax.rem(mine + i, count)))

    def over_others(step):
        loop(0, Z * CORES - CORES, lambda i: step(lax.rem(s - c + CORES + i, Z * CORES)))

    def rows(j):
        return pl.ds(pl.multiple_of(j * SLICE, SLICE), SLICE)

    def lanes(start, size):
        return pl.ds(pl.multiple_of(start, N), size)

    barrier = pltpu.get_barrier_semaphore()

    def greet(device):
        pl.semaphore_signal(barrier, inc=1, device_id=device, device_id_type=MESH)

    over(Z * CORES, s, lambda k: greet((g, k)))
    over(GROUPS, g, lambda k: greet((k, s)))

    padded = jnp.concatenate([a_ref[...], jnp.zeros((N - HEADS, T), F32)], axis=0)
    upto = (iota((T, T), 0) <= iota((T, T), 1)).astype(F32)
    cum_rows = nn(padded, upto, HIGH)
    cr[...] = cum_rows
    cum = cum_rows.T
    log = jnp.broadcast_to(cum[T - 1 : T, :], (8, N))
    logs[s] = log

    def log_copy(k):
        return copy(logs.at[s], logs.at[s], log_s.at[k], log_r.at[s], (g, k))

    def log_here(k):
        return copy(logs.at[k], logs.at[k], log_s.at[k], log_r.at[k], (g, k))

    left = iota((T, N), 1) < N // 2
    for i in range(HEADS // 2):
        cx[:, N * i : N * i + N] = jnp.where(left, cum[:, 2 * i : 2 * i + 1], cum[:, 2 * i + 1 : 2 * i + 2])

    def own(half, map_t, token_ref, weighted, state, weight):
        def step(k):
            at = lanes(half * HALF + k * CHUNK, CHUNK)
            part = (token_ref[:, at].astype(F32) * weight(at)).astype(BF16)
            weighted[:, at] = part
            state[half, :, lanes(k * CHUNK, CHUNK)] = nn(map_t, part)

        loop(0, HALF // CHUNK, step)

    def tails(at):
        return jnp.exp(cx[T - 1 : T, at] - cx[:, at])

    def leads(at):
        return jnp.exp(cx[:, at])

    w, r = w_ref[...], r_ref[...]
    w_t, r_t = w.T, r.T

    def half_copy(way, own_ref, theirs, j):
        return copy(own_ref.at[1 - c, rows(j)], theirs.at[rows(j)], h_s.at[way, j], h_r.at[way, j], other)

    def half_up(way, own_ref, theirs):
        loop(1, Z + 1, lambda i: half_copy(way, own_ref, theirs, lax.rem(z + i, Z)).start())

    own(1 - c, w_t, v_ref, vt, of, tails)
    own(c, w_t, v_ref, vt, of, tails)
    pl.semaphore_wait(barrier, Z * CORES - 1 + GROUPS - 1)
    log_copy(partner).start()
    half_up(0, of, xf)
    over_others(lambda k: log_copy(k).start())

    spread = (iota((N, HALF), 0) == iota((N, HALF), 1) // 64 + c * (HEADS // 2)).astype(F32)
    is_first = c == 0
    mine = nn(log, spread, HIGH)[0:1, :]
    log_here(partner).wait_recv()
    theirs = nn(logs[partner], spread, HIGH)[0:1, :]
    ex[0:1, :] = jnp.exp(jnp.where(is_first, mine, theirs))
    ex[1:2, :] = jnp.exp(jnp.where(is_first, theirs, mine))
    first, second = ex[0:1, :], ex[1:2, :]
    one = jnp.ones_like(first)

    def slices_up(way, own_ref, theirs, chip, up, a, b):
        def put(j):
            half_copy(way, own_ref, theirs, j).wait_recv()
            chip[rows(j), :] = a * own_ref[c, rows(j), :] + b * theirs[rows(j), :]

        def send(j):
            put(j)
            copy(chip.at[rows(j)], up.at[z], u_s.at[way, j], u_r.at[way, z], (g, j * CORES + c)).start()

        over(Z, z, send)
        put(z)
        up[z] = chip[rows(z), :]

    slices_up(
        0, of, xf, cf, uf, jnp.where(is_first, second, one), jnp.where(is_first, one, second)
    )

    own(1 - c, r_t, g_ref, gl, ob, leads)
    half_up(1, ob, xb)
    own(c, r_t, g_ref, gl, ob, leads)

    def glog_copy(k):
        return copy(glogs.at[g], glogs.at[g], glog_s.at[k], glog_r.at[g], (k, s))

    def glog_here(k):
        return copy(glogs.at[k], glogs.at[k], glog_s.at[k], glog_r.at[k], (k, s))

    over_others(lambda k: log_here(k).wait_recv())
    blocks = jnp.max(logs[...], axis=1)
    glogs[g] = jnp.broadcast_to(jnp.sum(blocks, axis=0, keepdims=True), (8, N))
    over(GROUPS, g, lambda k: glog_copy(k).start())

    slices_up(1, ob, xb, cb, ub, jnp.where(is_first, one, first), jnp.where(is_first, first, one))

    wide = nn(blocks, spread, HIGH)
    chip_of, place = iota((Z, Z * CORES), 1) // CORES, iota((Z, Z * CORES), 0)
    wz[...] = jnp.exp(nn((chip_of == place).astype(F32), wide, HIGH))
    ez[...] = jnp.exp(nn((chip_of < place).astype(F32), wide, HIGH))
    fz[...] = jnp.exp(nn((chip_of > place).astype(F32), wide, HIGH))
    over(GROUPS, g, lambda k: glog_here(k).wait_recv())
    wide = nn(jnp.max(glogs[...], axis=1), spread, HIGH)
    wg[...] = jnp.exp(wide)
    row_of, column_of = iota((8, GROUPS), 1) // SIDE, iota((8, GROUPS), 1) % SIDE
    place = iota((8, GROUPS), 0)
    beside = ((place == SIDE) & (column_of < x)) | ((place == SIDE + 1) & (column_of > x))
    picks = ((place < SIDE) & (row_of == place)) | ((row_of == y) & beside)
    wr[...] = jnp.exp(nn(picks.astype(F32), wide, HIGH))

    causal = iota((T, T), 0) >= iota((T, T), 1)
    scores = nt(r, w)
    sm[...] = jnp.zeros((T, T), F32)

    def intra(i):
        at = lanes(i * N, N)
        v, gr, two = v_ref[:, at], g_ref[:, at], cx[:, at]
        y_two, dx_two = [], []
        total = sm[...]
        for k in range(2):
            gap = two[:, 64 * k : 64 * k + 1] - cr[pl.ds(2 * i + k, 1), :]
            decay = jnp.exp(jnp.where(causal, gap, -jnp.inf))
            mixing = (scores * decay).astype(BF16)
            y_two.append(nn(mixing, v))
            dx_two.append(tn(mixing, gr))
            head = jnp.where(left if k == 0 else jnp.logical_not(left), gr, jnp.zeros_like(gr))
            total = total + nt(head, v) * decay
        sm[...] = total
        yi[:, at] = jnp.where(left, y_two[0], y_two[1])
        di[:, at] = jnp.where(left, dx_two[0], dx_two[1])

    loop(0, CUTS[0], intra)

    def up_here(way, chip, up, j):
        return copy(chip.at[rows(j)], up.at[j], u_s.at[way, j], u_r.at[way, j], (g, j * CORES + c))

    def total_copy(way, total, k):
        return copy(total.at[x], total.at[x], t_s.at[way, k], t_r.at[way, x], (y * SIDE + k, s))

    def total_here(way, total, k):
        return copy(total.at[k], total.at[k], t_s.at[way, k], t_r.at[way, k], (y * SIDE + k, s))

    def row_copy(way, total, k):
        return copy(total.at[y], total.at[y], r_s.at[way, k], r_r.at[way, y], (k * SIDE + x, s))

    def row_here(way, total, k):
        return copy(total.at[k], total.at[k], r_s.at[way, k], r_r.at[way, k], (k * SIDE + x, s))

    def down_copy(way, part, down, j):
        return copy(part.at[j], down.at[rows(z)], d_s.at[way, j], d_r.at[way, z], (g, j * CORES + c))

    def down_here(way, part, down, j):
        return copy(part.at[j], down.at[rows(j)], d_s.at[way, j], d_r.at[way, j], (g, j * CORES + c))

    empty = jnp.zeros((SLICE, HALF), F32)

    def ring(way, chip, up, part, total, order):
        over(Z, z, lambda j: up_here(way, chip, up, j).wait_recv())
        state = empty
        for j in order:
            part[j] = state
            state = wz[j : j + 1, :] * state + up[j]
        total[x] = state
        over(SIDE, x, lambda k: total_copy(way, total, k).start())

    def row(way, total, row_total, order):
        over(SIDE, x, lambda k: total_here(way, total, k).wait_recv())
        state, before = empty, empty
        for k in order:
            before = jnp.where(k == x, state, before)
            state = wg[pl.ds(y * SIDE + k, 1), :] * state + total[k]
        row_total[y] = state
        over(SIDE, y, lambda k: row_copy(way, row_total, k).start())
        total[SIDE] = before

    def column(way, part, total, row_total, down, decay, order):
        over(SIDE, y, lambda k: row_here(way, row_total, k).wait_recv())
        state, before = empty, empty
        for k in order:
            before = jnp.where(k == y, state, before)
            state = wr[k : k + 1, :] * state + row_total[k]
        state = wr[SIDE + way : SIDE + way + 1, :] * before + total[SIDE]

        def send(j):
            part[j] += decay[pl.ds(j, 1), :] * state
            down_copy(way, part, down, j).start()

        over(Z, z, send)
        down[rows(z), :] = part[z] + decay[pl.ds(z, 1), :] * state

    ahead, back = range(SIDE), range(SIDE - 1, -1, -1)
    ring(0, cf, uf, pf, tf, range(Z))
    loop(CUTS[0], CUTS[1], intra)
    row(0, tf, rf, ahead)
    loop(CUTS[1], CUTS[2], intra)
    ring(1, cb, ub, pb, tb, range(Z - 1, -1, -1))
    column(0, pf, tf, rf, df, ez, ahead)
    loop(CUTS[2], HEADS // 2, intra)
    row(1, tb, rb, back)
    half = sm[...].astype(BF16)
    dw[...] = tn(half, r)
    dr[...] = nn(half, w)
    column(1, pb, tb, rb, db, fz, back)

    def finish_f(side):
        def step(k):
            at, within = lanes(side * HALF + k * CHUNK, CHUNK), lanes(k * CHUNK, CHUNK)
            state = sf[side, :, within]
            state_half = state.astype(BF16)
            full = yi[:, at] + nn(r, state_half) * leads(at)
            yi[:, at] = g_ref[:, at].astype(F32) * full
            dr[...] += nt(gl[:, at], state_half)
            sf[side, :, within] = jnp.exp(cx[T - 1 : T, at]) * state + of[side, :, within]

        loop(0, HALF // CHUNK, step)

    last = iota((T, CHUNK), 0) == T - 1
    ch[...] = jnp.zeros((T, N), F32)

    def finish_b(side):
        def step(k):
            at, within = lanes(side * HALF + k * CHUNK, CHUNK), lanes(k * CHUNK, CHUNK)
            back_in = sb[side, :, within]
            back_half = back_in.astype(BF16)
            full = di[:, at] + nn(w, back_half) * tails(at)
            dv_ref[:, at] = full.astype(BF16)
            dw[...] += nt(vt[:, at], back_half)
            meet = jnp.sum(sf[side, :, within] * back_in, axis=0, keepdims=True)
            change = yi[:, at] - v_ref[:, at].astype(F32) * full + jnp.where(last, meet, 0.0)
            high = change.astype(BF16)
            low = (change - high.astype(F32)).astype(BF16)
            head = (side * HALF + k * CHUNK) // 64 + iota((CHUNK, N), 0) // 64
            picks = (iota((CHUNK, N), 1) == head).astype(F32).astype(BF16)
            ch[...] += nn(high, picks) + nn(low, picks)

        loop(0, HALF // CHUNK, step)

    over(Z, z, lambda j: down_here(0, pf, df, j).wait_recv())
    out_f = copy(kf, sf.at[c], x_s.at[0], x_r.at[0], other)

    @pl.when(is_first)
    def _():
        kf[...] = first * df[...] + of[c]
        sf[c] = df[...]

    @pl.when(jnp.logical_not(is_first))
    def _():
        kf[...] = df[...]
        sf[c] = first * df[...] + xf[...]

    out_f.start()
    finish_f(c)
    out_f.wait_recv()
    finish_f(1 - c)

    over(Z, z, lambda j: down_here(1, pb, db, j).wait_recv())
    out_b = copy(kb, sb.at[c], x_s.at[1], x_r.at[1], other)

    @pl.when(is_first)
    def _():
        kb[...] = db[...]
        sb[c] = second * db[...] + xb[...]

    @pl.when(jnp.logical_not(is_first))
    def _():
        kb[...] = second * db[...] + ob[c]
        sb[c] = db[...]

    out_b.start()
    finish_b(c)
    out_b.wait_recv()
    finish_b(1 - c)
    dw_ref[...] = dw[...].astype(BF16)
    dr_ref[...] = dr[...].astype(BF16)
    after = (iota((T, T), 0) >= iota((T, T), 1)).astype(F32)
    da_ref[...] = tn(ch[...], after, HIGH)[:HEADS, :]

    over(Z * CORES, s, lambda k: log_copy(k).wait_send())
    over(GROUPS, g, lambda k: glog_copy(k).wait_send())
    for way, chip, up, part, total, row_total, down in (
        (0, cf, uf, pf, tf, rf, df),
        (1, cb, ub, pb, tb, rb, db),
    ):
        over(Z, z, lambda j: up_here(way, chip, up, j).wait_send())
        over(SIDE, x, lambda k: total_copy(way, total, k).wait_send())
        over(SIDE, y, lambda k: row_copy(way, row_total, k).wait_send())
        over(Z, z, lambda j: down_copy(way, part, down, j).wait_send())
    for way, own_ref, theirs in ((0, of, xf), (1, ob, xb)):
        loop(0, Z, lambda j: half_copy(way, own_ref, theirs, j).wait_send())
    out_f.wait_send()
    out_b.wait_send()


def deliver(dv_in, dw_in, dr_in, da_in, dv_ref, dw_ref, dr_ref, da_ref, dv, dw, dr, da, sem):
    step = T // PIECES
    pieces = [pl.ds(i * step, step) for i in range(PIECES)]
    ways = [(dv_in.at[at], dv.at[at], dv_ref.at[at]) for at in pieces]
    ways += [(dw_in, dw, dw_ref), (dr_in, dr, dr_ref), (da_in, da, da_ref)]
    inward = [pltpu.make_async_copy(a, b, sem.at[0, i]) for i, (a, b, _) in enumerate(ways)]
    outward = [pltpu.make_async_copy(b, c, sem.at[1, i]) for i, (_, b, c) in enumerate(ways)]
    for each in inward:
        each.start()
    for one, two in zip(inward, outward):
        one.wait()
        two.start()
    for each in outward:
        each.wait()


def vmem(count):
    return [pl.BlockSpec(memory_space=pltpu.VMEM)] * count


def per_device(inputs, out_grad, input_map, output_map, log_decay):
    shape = jax.ShapeDtypeStruct
    whole = pltpu.VMEM((N, HALF), F32)
    both = pltpu.VMEM((CORES, N, HALF), F32)
    by_z = pltpu.VMEM((Z, SLICE, HALF), F32)
    by_side = pltpu.VMEM((SIDE + 1, SLICE, HALF), F32)
    dma = pltpu.SemaphoreType.DMA
    outs = (
        shape((T, WIDE), BF16),
        shape((T, N), BF16),
        shape((T, N), BF16),
        shape((HEADS, T), F32),
    )
    made = pl.pallas_call(
        block,
        out_shape=outs,
        in_specs=vmem(5),
        out_specs=tuple(vmem(4)),
        scratch_shapes=[
            pltpu.VMEM((N, T), F32),
            pltpu.VMEM((T, WIDE), F32),
            *([pltpu.VMEM((T, WIDE), BF16)] * 2),
            *([both] * 2),
            *([pltpu.VMEM((T, WIDE), F32)] * 2),
            pltpu.VMEM((T, T), F32),
            *([pltpu.VMEM((T, N), F32)] * 3),
            pltpu.VMEM((Z * CORES, 8, N), F32),
            pltpu.VMEM((GROUPS, 8, N), F32),
            *([whole] * 4),
            *([by_z] * 4),
            *([by_side] * 4),
            *([whole] * 4),
            *([both] * 2),
            *([pltpu.VMEM((Z, HALF), F32)] * 4),
            pltpu.VMEM((GROUPS, HALF), F32),
            pltpu.VMEM((8, HALF), F32),
            *([dma((GROUPS,))] * 4),
            *([dma((2,))] * 2),
            *([dma((2, Z))] * 4),
            *([dma((2, SIDE))] * 4),
            *([dma((2, Z))] * 2),
        ],
        compiler_params=pltpu.CompilerParams(
            collective_id=0, has_side_effects=True, vmem_limit_bytes=LIMIT
        ),
        name="block",
    )(inputs, out_grad, input_map, output_map, log_decay)
    anywhere = [pl.BlockSpec(memory_space=pl.ANY)] * 4
    return pl.pallas_call(
        deliver,
        out_shape=outs,
        in_specs=anywhere,
        out_specs=tuple(anywhere),
        scratch_shapes=[*(pltpu.VMEM(o.shape, o.dtype) for o in outs), dma((2, PIECES + 3))],
        compiler_params=pltpu.CompilerParams(vmem_limit_bytes=LIMIT),
        name="deliver",
    )(*made)


def solution(mesh):
    tokens = P(("grp", "seq"), None)
    rates = P(None, ("grp", "seq"))
    return jax.shard_map(
        per_device,
        mesh=mesh,
        in_specs=(tokens, tokens, tokens, tokens, rates),
        out_specs=(tokens, tokens, tokens, rates),
        check_vma=False,
    )
```

```python
import jax
import jax.numpy as jnp
from jax import lax
from jax.experimental import pallas as pl
from jax.experimental.pallas import tpu as pltpu
from jax.sharding import PartitionSpec as P

MESH = pl.DeviceIdType.MESH
HIGH = lax.Precision.HIGHEST
F32 = jnp.float32
BF16 = jnp.bfloat16
LIMIT = 56 * 2**20

T = 256
HEADS = 40
N = 128
WIDE = 2560
HALF = WIDE // 2
Z, CORES, GROUPS, SIDE = 8, 2, 16, 4
SLICE = N // Z
PIECES = 4
CHUNK = 256
CUTS = (14, 16, 18)


def nn(a, b, precision=None):
    return lax.dot_general(
        a, b, (((1,), (0,)), ((), ())), precision=precision, preferred_element_type=F32
    )


def nt(a, b, precision=None):
    return lax.dot_general(
        a, b, (((1,), (1,)), ((), ())), precision=precision, preferred_element_type=F32
    )


def tn(a, b, precision=None):
    return lax.dot_general(
        a, b, (((0,), (0,)), ((), ())), precision=precision, preferred_element_type=F32
    )


def iota(shape, dim):
    return lax.broadcasted_iota(jnp.int32, shape, dim)


def block(
    v_in, g_in, w_in, r_in, a_in, dv_ref, dw_ref, dr_ref, da_ref,
    v_ref, g_ref, w_ref, r_ref, a_ref, in_s, cr, cx, vt, gl, of, ob, yi, di, sm, dw, dr, ch,
    logs, glogs, xf, xb, cf, cb, uf, ub, pf, pb, tf, tb, rf, rb, df, db, kf, kb, sf, sb,
    wz, ez, fz, ex, wg, wr,
    log_s, log_r, glog_s, glog_r, x_s, x_r, h_s, h_r, u_s, u_r, t_s, t_r, r_s, r_r, d_s, d_r,
):
    g, s = lax.axis_index("grp"), lax.axis_index("seq")
    z, c = s // CORES, s % CORES
    y, x = g // SIDE, g % SIDE
    partner = z * CORES + 1 - c
    other = (g, partner)

    def copy(src, dst, send, recv, device):
        return pltpu.make_async_remote_copy(
            src_ref=src,
            dst_ref=dst,
            send_sem=send,
            recv_sem=recv,
            device_id=device,
            device_id_type=MESH,
        )

    def loop(first, last, step):
        def lap(i, carry):
            step(i)
            return carry

        lax.fori_loop(first, last, lap, 0)

    def over(count, mine, step):
        loop(1, count, lambda i: step(lax.rem(mine + i, count)))

    def over_others(step):
        loop(0, Z * CORES - CORES, lambda i: step(lax.rem(s - c + CORES + i, Z * CORES)))

    def rows(j):
        return pl.ds(pl.multiple_of(j * SLICE, SLICE), SLICE)

    def lanes(start, size):
        return pl.ds(pl.multiple_of(start, N), size)

    barrier = pltpu.get_barrier_semaphore()

    def greet(device):
        pl.semaphore_signal(barrier, inc=1, device_id=device, device_id_type=MESH)

    over(Z * CORES, s, lambda k: greet((g, k)))
    over(GROUPS, g, lambda k: greet((k, s)))
    arrays = ((a_in, a_ref), (v_in, v_ref), (w_in, w_ref), (r_in, r_ref), (g_in, g_ref))
    loads = [pltpu.make_async_copy(far, near, in_s.at[i]) for i, (far, near) in enumerate(arrays)]
    for each in loads:
        each.start()
    loads[0].wait()

    padded = jnp.concatenate([a_ref[...], jnp.zeros((N - HEADS, T), F32)], axis=0)
    upto = (iota((T, T), 0) <= iota((T, T), 1)).astype(F32)
    cum_rows = nn(padded, upto, HIGH)
    cr[...] = cum_rows
    cum = cum_rows.T
    log = jnp.broadcast_to(cum[T - 1 : T, :], (8, N))
    logs[s] = log

    def log_copy(k):
        return copy(logs.at[s], logs.at[s], log_s.at[k], log_r.at[s], (g, k))

    def log_here(k):
        return copy(logs.at[k], logs.at[k], log_s.at[k], log_r.at[k], (g, k))

    left = iota((T, N), 1) < N // 2
    for i in range(HEADS // 2):
        cx[:, N * i : N * i + N] = jnp.where(left, cum[:, 2 * i : 2 * i + 1], cum[:, 2 * i + 1 : 2 * i + 2])

    def own(half, map_t, token_ref, weighted, state, weight):
        def step(k):
            at = lanes(half * HALF + k * CHUNK, CHUNK)
            part = (token_ref[:, at].astype(F32) * weight(at)).astype(BF16)
            weighted[:, at] = part
            state[half, :, lanes(k * CHUNK, CHUNK)] = nn(map_t, part)

        loop(0, HALF // CHUNK, step)

    def tails(at):
        return jnp.exp(cx[T - 1 : T, at] - cx[:, at])

    def leads(at):
        return jnp.exp(cx[:, at])

    for each in loads[1:]:
        each.wait()
    w, r = w_ref[...], r_ref[...]
    w_t, r_t = w.T, r.T

    def half_copy(way, own_ref, theirs, j):
        return copy(own_ref.at[1 - c, rows(j)], theirs.at[rows(j)], h_s.at[way, j], h_r.at[way, j], other)

    def half_up(way, own_ref, theirs):
        loop(1, Z + 1, lambda i: half_copy(way, own_ref, theirs, lax.rem(z + i, Z)).start())

    own(1 - c, w_t, v_ref, vt, of, tails)
    own(c, w_t, v_ref, vt, of, tails)
    pl.semaphore_wait(barrier, Z * CORES - 1 + GROUPS - 1)
    log_copy(partner).start()
    half_up(0, of, xf)
    over_others(lambda k: log_copy(k).start())

    spread = (iota((N, HALF), 0) == iota((N, HALF), 1) // 64 + c * (HEADS // 2)).astype(F32)
    is_first = c == 0
    mine = nn(log, spread, HIGH)[0:1, :]
    log_here(partner).wait_recv()
    theirs = nn(logs[partner], spread, HIGH)[0:1, :]
    ex[0:1, :] = jnp.exp(jnp.where(is_first, mine, theirs))
    ex[1:2, :] = jnp.exp(jnp.where(is_first, theirs, mine))
    first, second = ex[0:1, :], ex[1:2, :]
    one = jnp.ones_like(first)

    def slices_up(way, own_ref, theirs, chip, up, a, b):
        def put(j):
            half_copy(way, own_ref, theirs, j).wait_recv()
            chip[rows(j), :] = a * own_ref[c, rows(j), :] + b * theirs[rows(j), :]

        def send(j):
            put(j)
            copy(chip.at[rows(j)], up.at[z], u_s.at[way, j], u_r.at[way, z], (g, j * CORES + c)).start()

        over(Z, z, send)
        put(z)
        up[z] = chip[rows(z), :]

    slices_up(
        0, of, xf, cf, uf, jnp.where(is_first, second, one), jnp.where(is_first, one, second)
    )

    own(1 - c, r_t, g_ref, gl, ob, leads)
    half_up(1, ob, xb)
    own(c, r_t, g_ref, gl, ob, leads)

    def glog_copy(k):
        return copy(glogs.at[g], glogs.at[g], glog_s.at[k], glog_r.at[g], (k, s))

    def glog_here(k):
        return copy(glogs.at[k], glogs.at[k], glog_s.at[k], glog_r.at[k], (k, s))

    over_others(lambda k: log_here(k).wait_recv())
    blocks = jnp.max(logs[...], axis=1)
    glogs[g] = jnp.broadcast_to(jnp.sum(blocks, axis=0, keepdims=True), (8, N))
    over(GROUPS, g, lambda k: glog_copy(k).start())

    slices_up(1, ob, xb, cb, ub, jnp.where(is_first, one, first), jnp.where(is_first, first, one))

    wide = nn(blocks, spread, HIGH)
    chip_of, place = iota((Z, Z * CORES), 1) // CORES, iota((Z, Z * CORES), 0)
    wz[...] = jnp.exp(nn((chip_of == place).astype(F32), wide, HIGH))
    ez[...] = jnp.exp(nn((chip_of < place).astype(F32), wide, HIGH))
    fz[...] = jnp.exp(nn((chip_of > place).astype(F32), wide, HIGH))
    over(GROUPS, g, lambda k: glog_here(k).wait_recv())
    wide = nn(jnp.max(glogs[...], axis=1), spread, HIGH)
    wg[...] = jnp.exp(wide)
    row_of, column_of = iota((8, GROUPS), 1) // SIDE, iota((8, GROUPS), 1) % SIDE
    place = iota((8, GROUPS), 0)
    beside = ((place == SIDE) & (column_of < x)) | ((place == SIDE + 1) & (column_of > x))
    picks = ((place < SIDE) & (row_of == place)) | ((row_of == y) & beside)
    wr[...] = jnp.exp(nn(picks.astype(F32), wide, HIGH))

    causal = iota((T, T), 0) >= iota((T, T), 1)
    scores = nt(r, w)
    sm[...] = jnp.zeros((T, T), F32)

    def intra(i):
        at = lanes(i * N, N)
        v, gr, two = v_ref[:, at], g_ref[:, at], cx[:, at]
        y_two, dx_two = [], []
        total = sm[...]
        for k in range(2):
            gap = two[:, 64 * k : 64 * k + 1] - cr[pl.ds(2 * i + k, 1), :]
            decay = jnp.exp(jnp.where(causal, gap, -jnp.inf))
            mixing = (scores * decay).astype(BF16)
            y_two.append(nn(mixing, v))
            dx_two.append(tn(mixing, gr))
            head = jnp.where(left if k == 0 else jnp.logical_not(left), gr, jnp.zeros_like(gr))
            total = total + nt(head, v) * decay
        sm[...] = total
        yi[:, at] = jnp.where(left, y_two[0], y_two[1])
        di[:, at] = jnp.where(left, dx_two[0], dx_two[1])

    loop(0, CUTS[0], intra)

    def up_here(way, chip, up, j):
        return copy(chip.at[rows(j)], up.at[j], u_s.at[way, j], u_r.at[way, j], (g, j * CORES + c))

    def total_copy(way, total, k):
        return copy(total.at[x], total.at[x], t_s.at[way, k], t_r.at[way, x], (y * SIDE + k, s))

    def total_here(way, total, k):
        return copy(total.at[k], total.at[k], t_s.at[way, k], t_r.at[way, k], (y * SIDE + k, s))

    def row_copy(way, total, k):
        return copy(total.at[y], total.at[y], r_s.at[way, k], r_r.at[way, y], (k * SIDE + x, s))

    def row_here(way, total, k):
        return copy(total.at[k], total.at[k], r_s.at[way, k], r_r.at[way, k], (k * SIDE + x, s))

    def down_copy(way, part, down, j):
        return copy(part.at[j], down.at[rows(z)], d_s.at[way, j], d_r.at[way, z], (g, j * CORES + c))

    def down_here(way, part, down, j):
        return copy(part.at[j], down.at[rows(j)], d_s.at[way, j], d_r.at[way, j], (g, j * CORES + c))

    empty = jnp.zeros((SLICE, HALF), F32)

    def ring(way, chip, up, part, total, order):
        over(Z, z, lambda j: up_here(way, chip, up, j).wait_recv())
        state = empty
        for j in order:
            part[j] = state
            state = wz[j : j + 1, :] * state + up[j]
        total[x] = state
        over(SIDE, x, lambda k: total_copy(way, total, k).start())

    def row(way, total, row_total, order):
        over(SIDE, x, lambda k: total_here(way, total, k).wait_recv())
        state, before = empty, empty
        for k in order:
            before = jnp.where(k == x, state, before)
            state = wg[pl.ds(y * SIDE + k, 1), :] * state + total[k]
        row_total[y] = state
        over(SIDE, y, lambda k: row_copy(way, row_total, k).start())
        total[SIDE] = before

    def column(way, part, total, row_total, down, decay, order):
        over(SIDE, y, lambda k: row_here(way, row_total, k).wait_recv())
        state, before = empty, empty
        for k in order:
            before = jnp.where(k == y, state, before)
            state = wr[k : k + 1, :] * state + row_total[k]
        state = wr[SIDE + way : SIDE + way + 1, :] * before + total[SIDE]

        def send(j):
            part[j] += decay[pl.ds(j, 1), :] * state
            down_copy(way, part, down, j).start()

        over(Z, z, send)
        down[rows(z), :] = part[z] + decay[pl.ds(z, 1), :] * state

    ahead, back = range(SIDE), range(SIDE - 1, -1, -1)
    ring(0, cf, uf, pf, tf, range(Z))
    loop(CUTS[0], CUTS[1], intra)
    row(0, tf, rf, ahead)
    loop(CUTS[1], CUTS[2], intra)
    ring(1, cb, ub, pb, tb, range(Z - 1, -1, -1))
    column(0, pf, tf, rf, df, ez, ahead)
    loop(CUTS[2], HEADS // 2, intra)
    row(1, tb, rb, back)
    half = sm[...].astype(BF16)
    dw[...] = tn(half, r)
    dr[...] = nn(half, w)
    column(1, pb, tb, rb, db, fz, back)

    def finish_f(side):
        def step(k):
            at, within = lanes(side * HALF + k * CHUNK, CHUNK), lanes(k * CHUNK, CHUNK)
            state = sf[side, :, within]
            state_half = state.astype(BF16)
            full = yi[:, at] + nn(r, state_half) * leads(at)
            yi[:, at] = g_ref[:, at].astype(F32) * full
            dr[...] += nt(gl[:, at], state_half)
            sf[side, :, within] = jnp.exp(cx[T - 1 : T, at]) * state + of[side, :, within]

        loop(0, HALF // CHUNK, step)

    last = iota((T, CHUNK), 0) == T - 1
    ch[...] = jnp.zeros((T, N), F32)

    def finish_b(side):
        def step(k):
            at, within = lanes(side * HALF + k * CHUNK, CHUNK), lanes(k * CHUNK, CHUNK)
            back_in = sb[side, :, within]
            back_half = back_in.astype(BF16)
            full = di[:, at] + nn(w, back_half) * tails(at)
            dv_ref[:, at] = full.astype(BF16)
            dw[...] += nt(vt[:, at], back_half)
            meet = jnp.sum(sf[side, :, within] * back_in, axis=0, keepdims=True)
            change = yi[:, at] - v_ref[:, at].astype(F32) * full + jnp.where(last, meet, 0.0)
            high = change.astype(BF16)
            low = (change - high.astype(F32)).astype(BF16)
            head = (side * HALF + k * CHUNK) // 64 + iota((CHUNK, N), 0) // 64
            picks = (iota((CHUNK, N), 1) == head).astype(F32).astype(BF16)
            ch[...] += nn(high, picks) + nn(low, picks)

        loop(0, HALF // CHUNK, step)

    over(Z, z, lambda j: down_here(0, pf, df, j).wait_recv())
    out_f = copy(kf, sf.at[c], x_s.at[0], x_r.at[0], other)

    @pl.when(is_first)
    def _():
        kf[...] = first * df[...] + of[c]
        sf[c] = df[...]

    @pl.when(jnp.logical_not(is_first))
    def _():
        kf[...] = df[...]
        sf[c] = first * df[...] + xf[...]

    out_f.start()
    finish_f(c)
    out_f.wait_recv()
    finish_f(1 - c)

    over(Z, z, lambda j: down_here(1, pb, db, j).wait_recv())
    out_b = copy(kb, sb.at[c], x_s.at[1], x_r.at[1], other)

    @pl.when(is_first)
    def _():
        kb[...] = db[...]
        sb[c] = second * db[...] + xb[...]

    @pl.when(jnp.logical_not(is_first))
    def _():
        kb[...] = second * db[...] + ob[c]
        sb[c] = db[...]

    out_b.start()
    finish_b(c)
    out_b.wait_recv()
    finish_b(1 - c)
    dw_ref[...] = dw[...].astype(BF16)
    dr_ref[...] = dr[...].astype(BF16)
    after = (iota((T, T), 0) >= iota((T, T), 1)).astype(F32)
    da_ref[...] = tn(ch[...], after, HIGH)[:HEADS, :]

    over(Z * CORES, s, lambda k: log_copy(k).wait_send())
    over(GROUPS, g, lambda k: glog_copy(k).wait_send())
    for way, chip, up, part, total, row_total, down in (
        (0, cf, uf, pf, tf, rf, df),
        (1, cb, ub, pb, tb, rb, db),
    ):
        over(Z, z, lambda j: up_here(way, chip, up, j).wait_send())
        over(SIDE, x, lambda k: total_copy(way, total, k).wait_send())
        over(SIDE, y, lambda k: row_copy(way, row_total, k).wait_send())
        over(Z, z, lambda j: down_copy(way, part, down, j).wait_send())
    for way, own_ref, theirs in ((0, of, xf), (1, ob, xb)):
        loop(0, Z, lambda j: half_copy(way, own_ref, theirs, j).wait_send())
    out_f.wait_send()
    out_b.wait_send()


def deliver(dv_in, dw_in, dr_in, da_in, dv_ref, dw_ref, dr_ref, da_ref, dv, dw, dr, da, sem):
    step = T // PIECES
    pieces = [pl.ds(i * step, step) for i in range(PIECES)]
    ways = [(dv_in.at[at], dv.at[at], dv_ref.at[at]) for at in pieces]
    ways += [(dw_in, dw, dw_ref), (dr_in, dr, dr_ref), (da_in, da, da_ref)]
    inward = [pltpu.make_async_copy(a, b, sem.at[0, i]) for i, (a, b, _) in enumerate(ways)]
    outward = [pltpu.make_async_copy(b, c, sem.at[1, i]) for i, (_, b, c) in enumerate(ways)]
    for each in inward:
        each.start()
    for one, two in zip(inward, outward):
        one.wait()
        two.start()
    for each in outward:
        each.wait()


def vmem(count):
    return [pl.BlockSpec(memory_space=pltpu.VMEM)] * count


def per_device(inputs, out_grad, input_map, output_map, log_decay):
    shape = jax.ShapeDtypeStruct
    whole = pltpu.VMEM((N, HALF), F32)
    both = pltpu.VMEM((CORES, N, HALF), F32)
    by_z = pltpu.VMEM((Z, SLICE, HALF), F32)
    by_side = pltpu.VMEM((SIDE + 1, SLICE, HALF), F32)
    dma = pltpu.SemaphoreType.DMA
    outs = (
        shape((T, WIDE), BF16),
        shape((T, N), BF16),
        shape((T, N), BF16),
        shape((HEADS, T), F32),
    )
    made = pl.pallas_call(
        block,
        out_shape=outs,
        in_specs=[pl.BlockSpec(memory_space=pl.ANY)] * 5,
        out_specs=tuple(vmem(4)),
        scratch_shapes=[
            *([pltpu.VMEM((T, WIDE), BF16)] * 2),
            *([pltpu.VMEM((T, N), BF16)] * 2),
            pltpu.VMEM((HEADS, T), F32),
            dma((5,)),
            pltpu.VMEM((N, T), F32),
            pltpu.VMEM((T, WIDE), F32),
            *([pltpu.VMEM((T, WIDE), BF16)] * 2),
            *([both] * 2),
            *([pltpu.VMEM((T, WIDE), F32)] * 2),
            pltpu.VMEM((T, T), F32),
            *([pltpu.VMEM((T, N), F32)] * 3),
            pltpu.VMEM((Z * CORES, 8, N), F32),
            pltpu.VMEM((GROUPS, 8, N), F32),
            *([whole] * 4),
            *([by_z] * 4),
            *([by_side] * 4),
            *([whole] * 4),
            *([both] * 2),
            *([pltpu.VMEM((Z, HALF), F32)] * 4),
            pltpu.VMEM((GROUPS, HALF), F32),
            pltpu.VMEM((8, HALF), F32),
            *([dma((GROUPS,))] * 4),
            *([dma((2,))] * 2),
            *([dma((2, Z))] * 4),
            *([dma((2, SIDE))] * 4),
            *([dma((2, Z))] * 2),
        ],
        compiler_params=pltpu.CompilerParams(
            collective_id=0, has_side_effects=True, vmem_limit_bytes=LIMIT
        ),
        name="block",
    )(inputs, out_grad, input_map, output_map, log_decay)
    anywhere = [pl.BlockSpec(memory_space=pl.ANY)] * 4
    return pl.pallas_call(
        deliver,
        out_shape=outs,
        in_specs=anywhere,
        out_specs=tuple(anywhere),
        scratch_shapes=[*(pltpu.VMEM(o.shape, o.dtype) for o in outs), dma((2, PIECES + 3))],
        compiler_params=pltpu.CompilerParams(vmem_limit_bytes=LIMIT),
        name="deliver",
    )(*made)


def solution(mesh):
    tokens = P(("grp", "seq"), None)
    rates = P(None, ("grp", "seq"))
    return jax.shard_map(
        per_device,
        mesh=mesh,
        in_specs=(tokens, tokens, tokens, tokens, rates),
        out_specs=(tokens, tokens, tokens, rates),
        check_vma=False,
    )
```
